128 devices in a mesh: tm: 8 (over x, core), row: 4 (over z), col: 4 (over y).
Axes of the slice: x: 4, y: 4, z: 4, core: 2. Of those that a mesh axis runs over, the one named last changes fastest.
Arguments:
- frames_in: bfloat16 [64, 32, 640, 128], P('tm', 'row', 'col'), may hold values from -6 to 6
- clip_frames: int32 [4], replicated, may hold values from 1 to 32, 64 in all
- conv_weight: bfloat16 [3, 3, 3, 128, 256], replicated, may hold values from -0.109375 to 0.109375
- norm_gain: float32 [256], replicated, may hold values from 0.1 to 1.9
- norm_shift: float32 [256], replicated, may hold values from -3 to 3
Outputs:
- activated: bfloat16 [64, 32, 640, 256], P('tm', 'row', 'col')
The draws below stay inside these ranges and needn't reach their ends.
Inputs may be any that keep to these rules, and one draw needn't show every extreme that they name: `clip_frames`: every clip has at least one frame; the longest has exactly 32.
All inputs are finite; a program needn't handle non-finite values.
Results may differ from the reference program's by a relative error of at most 0.0005.
Values may be sent and summed in bfloat16 or wider, within the bound.
No kernel may reach another device: no remote copies, remote signals or barrier semaphores. Data moves between devices by JAX's collectives and lax.ppermute only.
A program may use at most 128 MiB of HBM per device.

```python
import math
import jax
import jax.numpy as jnp
import numpy as np
from jax import lax

CIN = 128
COUT = 256
GROUPS = 32
CLIPS = 4
FRAMES = 64
MOST = 32
NH = 32
NW = 640


def steps_of(stream_key, shape, shards, smallest, largest):
    loudness = 1.0
    for axis_at, blocks in shards:
        heights = jax.random.uniform(jax.random.fold_in(jax.random.fold_in(stream_key, 6), axis_at), (blocks,), jnp.float32, smallest / len(shards), largest / len(shards))
        loudness = loudness * jnp.repeat(jnp.exp(heights), shape[axis_at] // blocks).reshape((-1,) + (1,) * (len(shape) - 1 - axis_at))
    return loudness


def length_profile(count, total, limit, skew):
    portions = [(1 << 20) // math.isqrt(standing ** skew) + 1 for standing in range(2, count + 1)]
    surplus, counts = total - limit - (count - 1), [1] * (count - 1)
    while surplus > 0:
        candidates = [i for i in range(count - 1) if counts[i] < limit]
        pool, remaining = sum([portions[i] for i in candidates]), surplus
        for i in candidates:
            addition = min(limit - counts[i], max(1, remaining * portions[i] // pool), surplus)
            counts[i] = counts[i] + addition
            surplus = surplus - addition
    return np.array([limit] + counts)


def uneven_parts(key, amount, total, limit, slope):
    if amount == 2:
        one = jax.random.randint(key, (), max(1, total - limit), min(limit, total - 1) + 1)
        return jnp.stack([one, total - one])
    tallies = jnp.asarray(length_profile(amount, total, limit, slope), jnp.int32)
    pairs = (amount - 1) // 2
    donor, taker = tallies[1:1 + 2 * pairs:2], tallies[2:2 + 2 * pairs:2]
    slack = jnp.minimum(donor - 1, limit - taker)
    shifted = jax.random.randint(jax.random.fold_in(key, 1), (pairs,), 0, 1 << 20) % (slack + 1)
    tallies = tallies.at[1:1 + 2 * pairs:2].set(donor - shifted).at[2:2 + 2 * pairs:2].set(taker + shifted)
    return tallies[jax.random.permutation(jax.random.fold_in(key, 2), amount)]


def scatter_about(rng, dims, spread, bound, cuts=(), held_as=jnp.bfloat16):
    drawn = spread * jax.random.normal(rng, dims, jnp.float32)
    if cuts:
        drawn = drawn * steps_of(rng, dims, cuts, -0.22, 0.18)
    return jnp.clip(drawn, -bound, bound).astype(held_as)


def setup_inputs(seed: int = 0) -> dict:
    key_of = jax.random.split(jax.random.key(seed), 6)
    return {
        "frames_in": scatter_about(key_of[0], (FRAMES, NH, NW, CIN), 1.0, 6.0, ((0, 8), (1, 4), (2, 4))),
        "clip_frames": uneven_parts(key_of[1], CLIPS, FRAMES, MOST, 2).astype(jnp.int32),
        "conv_weight": scatter_about(key_of[2], (3, 3, 3, CIN, COUT), (27 * CIN) ** -0.5, 0.109375),
        "norm_gain": jnp.clip(1.0 + 0.18 * jax.random.normal(key_of[3], (COUT,), jnp.float32), 0.1, 1.9),
        "norm_shift": scatter_about(key_of[4], (COUT,), 0.5, 3.0, (), jnp.float32),
    }


def plane_conv(frames, kernel):
    return lax.conv_general_dilated(frames, kernel, (1, 1), 'VALID', dimension_numbers=('NHWC', 'HWIO', 'NHWC'), preferred_element_type=jnp.float32)

def reference(frames_in, clip_frames, conv_weight, norm_gain, norm_shift):
    total = frames_in.shape[0]
    starts = (jnp.cumsum(clip_frames) - clip_frames).astype(jnp.int32)
    glob = jnp.arange(total, dtype=jnp.int32)
    member = (glob[:, None] >= starts[None, :]).astype(jnp.int32)
    clip_of = (lax.optimization_barrier(jnp.sum(member, axis=1)) - 1).astype(jnp.int32)
    onehot = clip_of[:, None] == jnp.arange(CLIPS, dtype=jnp.int32)[None, :]
    start_of = lax.optimization_barrier(jnp.sum(onehot.astype(jnp.int32) * starts[None, :], axis=1)).astype(jnp.int32)
    padded = jnp.pad(frames_in, ((0, 0), (1, 1), (1, 1), (0, 0)), mode='edge')
    conv = jnp.zeros((total, NH, NW, COUT), jnp.float32)
    for tap in range(3):
        source = jnp.maximum(glob - 2 + tap, start_of).astype(jnp.int32)
        conv = conv + plane_conv(jnp.take(padded, source, axis=0), conv_weight[tap])
    share = COUT // GROUPS
    onef = onehot.astype(jnp.float32)
    count = (clip_frames.astype(jnp.float32) * (NH * NW * share))[:, None]
    frame_sums = lax.optimization_barrier(jnp.sum(conv.reshape(total, NH * NW, GROUPS, share), axis=(1, 3)))
    mean = jnp.dot(onef.T, frame_sums, precision=lax.Precision.HIGHEST) / count
    mean_frames = jnp.dot(onef, mean, precision=lax.Precision.HIGHEST)
    centred = conv.reshape(total, NH * NW, GROUPS, share) - mean_frames[:, None, :, None]
    frame_sq = lax.optimization_barrier(jnp.sum(centred * centred, axis=(1, 3)))
    var = jnp.dot(onef.T, frame_sq, precision=lax.Precision.HIGHEST) / count
    scale_frames = jnp.dot(onef, lax.rsqrt(var + 1e-06), precision=lax.Precision.HIGHEST)
    normed = (centred * scale_frames[:, None, :, None]).reshape(total, NH, NW, COUT)
    return jax.nn.silu(normed * norm_gain + norm_shift).astype(jnp.bfloat16)
```

```python
import functools

import jax
import jax.numpy as jnp
from jax import lax
from jax.experimental import pallas as pl
from jax.experimental.pallas import tpu as pltpu
from jax.sharding import PartitionSpec as P

COUT = 256
GROUPS = 32
CLIPS = 4
SHARE = COUT // GROUPS
F, H, W, C = 8, 8, 160, 128
C3 = 3 * C
BF, F32 = jnp.bfloat16, jnp.float32
VMEM = pl.BlockSpec(memory_space=pltpu.VMEM)
SMEM = pl.BlockSpec(memory_space=pltpu.SMEM)
ANY = pl.BlockSpec(memory_space=pl.ANY)
HIGH = lax.Precision.HIGHEST


def clip_starts(frames_ref):
    starts = [0]
    for c in range(CLIPS - 1):
        starts.append(starts[-1] + frames_ref[c])
    return starts


def source(starts, first, f, k):
    g = first + f
    start = 0
    for s in starts[1:]:
        start = jnp.where(g >= s, s, start)
    return jnp.maximum(g - 2 + k, start) - first


def clip_index(starts, g):
    c = (g >= starts[1]).astype(jnp.int32)
    for s in starts[2:]:
        c = c + (g >= s).astype(jnp.int32)
    return c


def edges():
    row, col = lax.axis_index("row"), lax.axis_index("col")
    return row == 0, row == lax.axis_size("row") - 1, col == 0, col == lax.axis_size("col") - 1


def put_columns(xc, at, x, low, high):
    xc[(*at, slice(None), slice(0, C))] = jnp.concatenate([low, x[:, :-1]], axis=1)
    xc[(*at, slice(None), slice(C, 2 * C))] = x
    xc[(*at, slice(None), slice(2 * C, 3 * C))] = jnp.concatenate([x[:, 1:], high], axis=1)


def own_columns(xc, x_ref, frames):
    _, _, left, right = edges()

    def step(f, carry):
        x = x_ref[f]
        low = jnp.where(left, x[:, :1], jnp.zeros_like(x[:, :1]))
        high = jnp.where(right, x[:, -1:], jnp.zeros_like(x[:, -1:]))
        put_columns(xc, (f + 2, slice(1, H + 1)), x, low, high)
        return carry

    lax.fori_loop(frames[0], frames[1], step, 0)


def inner_taps(xc, w_ref, sources):
    rows = H - 2
    parts = [
        xc[s, 1 + dy : 1 + dy + rows].reshape(rows * W, C3) for _, s in sources for dy in range(3)
    ]
    k0 = sources[0][0]
    weights = w_ref[k0 * 3 * C3 : (k0 + len(sources)) * 3 * C3]
    out = jnp.dot(jnp.concatenate(parts, axis=1), weights, preferred_element_type=F32)
    return out.reshape(rows, W, COUT)


def first_kernel(frames_ref, x_ref, w_ref, xc, conv):
    first = lax.axis_index("tm") * F
    starts = clip_starts(frames_ref)
    own_columns(xc, x_ref, (0, 5))
    src = lambda f, k: source(starts, first, f, k) + 2
    conv[0, 1 : H - 1] = inner_taps(xc, w_ref, [(2, 2)])
    conv[1, 1 : H - 1] = inner_taps(xc, w_ref, [(1, src(1, 1)), (2, 3)])

    def step(f, carry):
        conv[f, 1 : H - 1] = inner_taps(xc, w_ref, [(0, src(f, 0)), (1, src(f, 1)), (2, f + 2)])
        return carry

    lax.fori_loop(2, 5, step, 0)


def second_kernel(frames_ref, x_ref, w_ref, xc_in, conv_in, xc, conv):
    del xc_in, conv_in
    first = lax.axis_index("tm") * F
    starts = clip_starts(frames_ref)
    own_columns(xc, x_ref, (5, 8))
    src = lambda f, k: source(starts, first, f, k) + 2

    def step(f, carry):
        conv[f, 1 : H - 1] = inner_taps(xc, w_ref, [(0, src(f, 0)), (1, src(f, 1)), (2, f + 2)])
        return carry

    lax.fori_loop(5, 8, step, 0)


def strip_kernel(x_ref, before, above, below, above_before, below_before, low_out, high_out):
    top, bottom, _, _ = edges()
    for out, at, pick in ((low_out, 0, 0), (high_out, W - 16, 15)):
        tile = lambda ref, f, r: ref[f, r, at : at + 16].astype(F32)[pick : pick + 1]
        for f in range(F + 2):
            own, over, under, g = (
                (before, above_before, below_before, f) if f < 2 else (x_ref, above, below, f - 2)
            )
            rows = [tile(own, g, r) for r in range(H)]
            head = jnp.where(top, rows[0], tile(over, g, 0))
            tail = jnp.where(bottom, rows[-1], tile(under, g, 0))
            pad = jnp.zeros((16 - H - 2, C), F32)
            out[f] = jnp.concatenate([head, *rows, tail, pad], axis=0).astype(BF)


def outer_kernel(
    frames_ref,
    w_ref,
    before,
    above,
    below,
    above_before,
    below_before,
    low_ref,
    high_ref,
    xc_in,
    conv_in,
    xc,
    conv,
    stats,
):
    del xc_in, conv_in
    first = lax.axis_index("tm") * F
    starts = clip_starts(frames_ref)
    top, bottom, left, right = edges()
    src = lambda f, k: source(starts, first, f, k) + 2
    tile_row = lax.broadcasted_iota(jnp.int32, (16, C), 0)

    def ends(ref, f, r):
        return ref[f].astype(F32)[r : r + 1]

    def fill_row(f, r, x):
        low = jnp.where(left, x[:1].astype(F32), ends(low_ref, f, r)).astype(BF)
        high = jnp.where(right, x[-1:].astype(F32), ends(high_ref, f, r)).astype(BF)
        put_columns(xc, (f, slice(r, r + 1)), x[None], low[None], high[None])

    for f in range(2):
        rows = [before[f, r] for r in range(H)]
        head = jnp.where(top, rows[0], above_before[f, 0])
        tail = jnp.where(bottom, rows[-1], below_before[f, 0])
        for r, x in enumerate([head, *rows, tail]):
            fill_row(f, r, x)
    for f in range(F):
        for r, edge, halo, own in ((0, top, above, 1), (H + 1, bottom, below, H)):
            fill_row(f + 2, r, jnp.where(edge, xc[f + 2, own, :, C : 2 * C], halo[f, 0]))
        for r in range(1, H + 1) if f < 2 else (1, 2, H - 1, H):
            low = xc[f + 2, r, 0:16, 0:C].astype(F32)
            low = jnp.where((tile_row == 0) & ~left, ends(low_ref, f + 2, r), low)
            xc[f + 2, r, 0:16, 0:C] = low.astype(BF)
            high = xc[f + 2, r, W - 16 : W, 2 * C : C3].astype(F32)
            high = jnp.where((tile_row == 15) & ~right, ends(high_ref, f + 2, r), high)
            xc[f + 2, r, W - 16 : W, 2 * C : C3] = high.astype(BF)

    def outer_rows(f, carry):
        parts = []
        for k in range(3):
            s = src(f, k)
            for dy in range(3):
                parts.append(jnp.concatenate([xc[s, dy], xc[s, H - 1 + dy]], axis=0))
        out = jnp.dot(jnp.concatenate(parts, axis=1), w_ref[...], preferred_element_type=F32)
        conv[f, 0] = out[:W]
        conv[f, H - 1] = out[W:]
        return carry

    lax.fori_loop(0, F, outer_rows, 0)
    conv[0, 1 : H - 1] += inner_taps(xc, w_ref, [(0, src(0, 0)), (1, src(0, 1))])
    conv[1, 1 : H - 1] += inner_taps(xc, w_ref, [(0, src(1, 0))])

    rows = H - 2
    sublane = lax.broadcasted_iota(jnp.int32, (8, COUT), 0)
    for ref, dx, at, pick in ((low_ref, 0, 0, 0), (high_ref, 2, W - 8, 7)):
        lhs = []
        for f in range(F):
            parts = []
            for k in range(3):
                strip = jnp.zeros((16, C), F32) if f + k < 2 else ref[src(f, k)].astype(F32)
                parts += [strip[1 + dy : 1 + dy + 8] for dy in range(3)]
            lhs.append(jnp.concatenate(parts, axis=1))
        lhs = jnp.concatenate(lhs, axis=0).astype(BF)
        weights = jnp.concatenate(
            [w_ref[(t * 3 + dx) * C : (t * 3 + dx + 1) * C] for t in range(9)], axis=0
        )
        out = jnp.dot(lhs, weights, preferred_element_type=F32)
        for f in range(F):
            for r in range(rows):
                add = out[f * 8 + r : f * 8 + r + 1]
                conv[f, 1 + r, at : at + 8] += jnp.where(sublane == pick, add, 0.0)

    def sums(f, carry):
        return jnp.where(
            frame_row == f, jnp.sum(conv[f].reshape(H * W, COUT), axis=0, keepdims=True), carry
        )

    frame_row = lax.broadcasted_iota(jnp.int32, (F, COUT), 0)
    zero = jnp.zeros((F, COUT), F32)
    totals = lax.fori_loop(0, F, sums, zero)
    channel = lax.broadcasted_iota(jnp.int32, (COUT, COUT), 0) // SHARE
    same_group = channel == lax.broadcasted_iota(jnp.int32, (COUT, COUT), 1) // SHARE
    grouped = jnp.dot(totals, same_group.astype(F32), precision=HIGH, preferred_element_type=F32)
    clip = clip_index(starts, first + frame_row)
    clip_sum, clip_count = zero, zero
    for f in range(F):
        same = clip == clip[f : f + 1]
        clip_sum = clip_sum + jnp.where(same, grouped[f : f + 1], 0.0)
        clip_count = clip_count + jnp.where(same, float(H * W * SHARE), 0.0)
    centre = clip_sum / clip_count

    def squares(f, carry):
        mean = jnp.sum(jnp.where(frame_row == f, centre, 0.0), axis=0, keepdims=True)
        off = conv[f].reshape(H * W, COUT) - mean
        return jnp.where(frame_row == f, jnp.sum(off * off, axis=0, keepdims=True), carry)

    spread = lax.fori_loop(0, F, squares, zero)
    lane = lax.broadcasted_iota(jnp.int32, (COUT, CLIPS * GROUPS), 1)
    pick = lax.broadcasted_iota(jnp.int32, (COUT, CLIPS * GROUPS), 0) // SHARE == lane % GROUPS
    mine = lax.broadcasted_iota(jnp.int32, (F, CLIPS * GROUPS), 1) // GROUPS
    mine = mine == clip[:, : CLIPS * GROUPS]
    for i, value in enumerate((totals, spread)):
        packed = jnp.dot(value, pick.astype(F32), precision=HIGH, preferred_element_type=F32)
        packed = jnp.sum(jnp.where(mine, packed, 0.0), axis=0, keepdims=True)
        stats[:, i * CLIPS * GROUPS : (i + 1) * CLIPS * GROUPS] = packed


def norm_kernel(cells, frames_ref, all_ref, gain, shift, conv, out_ref, held, sems):
    first = lax.axis_index("tm") * F
    starts = clip_starts(frames_ref)
    lanes = CLIPS * GROUPS
    count = all_ref.shape[0]
    value = all_ref[...]
    total, spread = value[:, :lanes], value[:, lanes:]
    which = lax.broadcasted_iota(jnp.int32, (count, lanes), 1) // GROUPS
    begin, length = jnp.zeros_like(which), jnp.zeros_like(which)
    for c in range(CLIPS):
        begin = jnp.where(which == c, starts[c], begin)
        length = jnp.where(which == c, frames_ref[c], length)
    slab = lax.broadcasted_iota(jnp.int32, (count, lanes), 0) // (count // lax.axis_size("tm")) * F
    part = jnp.minimum(slab + F, begin + length) - jnp.maximum(slab, begin)
    part = jnp.maximum(part, 0).astype(F32) * float(H * W * SHARE)
    whole = length[:1].astype(F32) * float(cells * SHARE)
    mean = jnp.sum(total, axis=0, keepdims=True) / whole
    off = total / jnp.maximum(part, 1.0) - mean
    var = jnp.sum(spread + part * (off * off), axis=0, keepdims=True) / whole
    var = var + 1e-06
    scale = lax.rsqrt(var)
    scale = scale * (1.5 - 0.5 * var * scale * scale)

    frame_row = lax.broadcasted_iota(jnp.int32, (F, lanes), 0)
    mine = clip_index(starts, first + frame_row)
    mine = mine == lax.broadcasted_iota(jnp.int32, (F, lanes), 1) // GROUPS
    lane = lax.broadcasted_iota(jnp.int32, (lanes, COUT), 0) % GROUPS
    spreadout = (lane == lax.broadcasted_iota(jnp.int32, (lanes, COUT), 1) // SHARE).astype(F32)

    def per_channel(v):
        v = jnp.where(mine, v, 0.0)
        return jnp.dot(v, spreadout, precision=HIGH, preferred_element_type=F32)

    mean, scale = per_channel(mean), per_channel(scale) * (0.5 * gain[...])
    half = 0.5 * shift[...]

    copies = []
    for f in range(F):

        def row(h, carry):
            u = (conv[f, h] - mean[f : f + 1]) * scale[f : f + 1] + half
            held[f, h] = (u + u * jnp.tanh(u)).astype(BF)
            return carry

        lax.fori_loop(0, H, row, 0)
        copy = pltpu.make_async_copy(held.at[f], out_ref.at[f], sems.at[f])
        copy.start()
        copies.append(copy)
    for copy in copies:
        copy.wait()


def params(mib):
    return pltpu.CompilerParams(vmem_limit_bytes=mib << 20)


def cost(flops, moved):
    return pl.CostEstimate(flops=flops, bytes_accessed=moved, transcendentals=0)


def shards(frames_in, clip_frames, conv_weight, norm_gain, norm_shift):
    n_tm, n_row, n_col = (lax.axis_size(a) for a in ("tm", "row", "col"))
    weights = conv_weight.reshape(27 * C, COUT)
    tail = frames_in[F - 2 :]
    before = lax.ppermute(tail, "tm", [(i, i + 1) for i in range(n_tm - 1)])
    down = [(i, i + 1) for i in range(n_row - 1)]
    up = [(i + 1, i) for i in range(n_row - 1)]
    above = lax.ppermute(frames_in[:, H - 1 :], "row", down)
    below = lax.ppermute(frames_in[:, :1], "row", up)

    def diagonal(pairs):
        return [
            (t * n_row + i, (t + 1) * n_row + j) for t in range(n_tm - 1) for i, j in pairs
        ]

    above_before = lax.ppermute(tail[:, H - 1 :], ("tm", "row"), diagonal(down))
    below_before = lax.ppermute(tail[:, :1], ("tm", "row"), diagonal(up))

    xc_shape = pltpu.VMEM((F + 2, H + 2, W, C3), BF)
    conv_shape = pltpu.VMEM((F, H, W, COUT), F32)
    macs = 6 * W * 3 * C3 * COUT
    xc, conv = pl.pallas_call(
        first_kernel,
        out_shape=(xc_shape, conv_shape),
        in_specs=[SMEM, VMEM, VMEM],
        out_specs=(VMEM, VMEM),
        compiler_params=params(20),
        cost_estimate=cost(2 * 12 * macs, 5 << 20),
        name="inner_first",
    )(clip_frames, frames_in, weights)
    low, high = pl.pallas_call(
        strip_kernel,
        out_shape=[jax.ShapeDtypeStruct((F + 2, 16, C), BF)] * 2,
        in_specs=[VMEM] * 6,
        out_specs=[VMEM] * 2,
        compiler_params=params(20),
        cost_estimate=cost(1 << 20, 1 << 16),
        name="strips",
    )(frames_in, before, above, below, above_before, below_before)
    from_left = lax.ppermute(high, "col", [(i, i + 1) for i in range(n_col - 1)])
    from_right = lax.ppermute(low, "col", [(i + 1, i) for i in range(n_col - 1)])
    xc, conv = pl.pallas_call(
        second_kernel,
        out_shape=(xc_shape, conv_shape),
        in_specs=[SMEM, VMEM, VMEM, VMEM, VMEM],
        out_specs=(VMEM, VMEM),
        input_output_aliases={3: 0, 4: 1},
        compiler_params=params(20),
        cost_estimate=cost(2 * 9 * macs, 5 << 20),
        name="inner_second",
    )(clip_frames, frames_in, weights, xc, conv)
    _, conv, stats = pl.pallas_call(
        outer_kernel,
        out_shape=(xc_shape, conv_shape, jax.ShapeDtypeStruct((1, 2 * CLIPS * GROUPS), F32)),
        in_specs=[SMEM] + [VMEM] * 10,
        out_specs=(VMEM, VMEM, VMEM),
        input_output_aliases={9: 0, 10: 1},
        compiler_params=params(24),
        cost_estimate=cost(2 * 12 * macs, 5 << 20),
        name="outer",
    )(
        clip_frames,
        weights,
        before,
        above,
        below,
        above_before,
        below_before,
        from_left,
        from_right,
        xc,
        conv,
    )
    count = n_tm * n_row * n_col
    every = jnp.broadcast_to(stats[None], (count, *stats.shape))
    every = lax.all_to_all(every, ("tm", "row", "col"), 0, 0).reshape(count, -1)
    return pl.pallas_call(
        functools.partial(norm_kernel, H * n_row * W * n_col),
        out_shape=jax.ShapeDtypeStruct((F, H, W, COUT), BF),
        in_specs=[SMEM] + [VMEM] * 4,
        out_specs=ANY,
        scratch_shapes=[pltpu.VMEM((F, H, W, COUT), BF), pltpu.SemaphoreType.DMA((F,))],
        compiler_params=params(24),
        cost_estimate=cost(1 << 24, 16 << 20),
        name="norm_silu",
    )(clip_frames, every, norm_gain[None], norm_shift[None], conv)


def solution(mesh):
    return jax.shard_map(
        shards,
        mesh=mesh,
        in_specs=(P("tm", "row", "col", None), P(), P(), P(), P()),
        out_specs=P("tm", "row", "col", None),
        check_vma=False,
    )
```

```python
import functools

import jax
import jax.numpy as jnp
from jax import lax
from jax.experimental import pallas as pl
from jax.experimental.pallas import tpu as pltpu
from jax.sharding import PartitionSpec as P

COUT = 256
GROUPS = 32
CLIPS = 4
SHARE = COUT // GROUPS
F, H, W, C = 8, 8, 160, 128
C3 = 3 * C
BF, F32 = jnp.bfloat16, jnp.float32
VMEM = pl.BlockSpec(memory_space=pltpu.VMEM)
SMEM = pl.BlockSpec(memory_space=pltpu.SMEM)
HBM = pl.BlockSpec(memory_space=pltpu.HBM)
HIGH = lax.Precision.HIGHEST


def clip_starts(frames_ref):
    starts = [0]
    for c in range(CLIPS - 1):
        starts.append(starts[-1] + frames_ref[c])
    return starts


def source(starts, first, f, k):
    g = first + f
    start = 0
    for s in starts[1:]:
        start = jnp.where(g >= s, s, start)
    return jnp.maximum(g - 2 + k, start) - first


def clip_index(starts, g):
    c = (g >= starts[1]).astype(jnp.int32)
    for s in starts[2:]:
        c = c + (g >= s).astype(jnp.int32)
    return c


def edges():
    row, col = lax.axis_index("row"), lax.axis_index("col")
    return row == 0, row == lax.axis_size("row") - 1, col == 0, col == lax.axis_size("col") - 1


def pack_kernel(x_ref, tail, top_row, bottom_row, tail_top, tail_bottom, sems):
    pairs = (
        (x_ref.at[:, H - 1], bottom_row),
        (x_ref.at[:, 0], top_row),
        (x_ref.at[F - 2 :], tail),
        (x_ref.at[F - 2 :, H - 1], tail_bottom),
        (x_ref.at[F - 2 :, 0], tail_top),
    )
    copies = [pltpu.make_async_copy(a, b, sems.at[i]) for i, (a, b) in enumerate(pairs)]
    for copy in copies:
        copy.start()
    for copy in copies:
        copy.wait()


def put_columns(xc, at, x):
    _, _, left, right = edges()
    low = jnp.where(left, x[:, :1], jnp.zeros_like(x[:, :1]))
    high = jnp.where(right, x[:, -1:], jnp.zeros_like(x[:, -1:]))
    xc[(*at, slice(None), slice(None), slice(0, C))] = jnp.concatenate([low, x[:, :-1]], axis=1)
    xc[(*at, slice(None), slice(None), slice(C, 2 * C))] = x
    xc[(*at, slice(None), slice(None), slice(2 * C, 3 * C))] = jnp.concatenate([x[:, 1:], high], axis=1)


def time_weights(w_ref, taps):
    return w_ref[taps[0] * 3 * C3 : (taps[-1] + 1) * 3 * C3]


def inner_taps(frames, row, rows, w_ref, taps):
    parts = [
        frame[row - 1 + dy : row - 1 + dy + rows].reshape(rows * W, C3)
        for frame in frames
        for dy in range(3)
    ]
    lhs = jnp.concatenate(parts, axis=1)
    out = jnp.dot(lhs, time_weights(w_ref, taps), preferred_element_type=F32)
    return out.reshape(rows, W, COUT)


def cell_sum(v):
    sublane = lax.broadcasted_iota(jnp.int32, (1, 8, COUT), 1)
    v = jnp.concatenate(
        [
            jnp.where(sublane > 0, v[:, :8], 0.0),
            v[:, 8:-8],
            jnp.where(sublane < 7, v[:, -8:], 0.0),
        ],
        axis=1,
    )
    return jnp.sum(v.reshape(-1, COUT), axis=0, keepdims=True)


def add_stats(stats, f, v):
    off = v - stats[f, 0:1]
    stats[f, 1:2] += cell_sum(off)
    stats[f, 2:3] += cell_sum(off * off)


def start_stats(stats, f, v):
    stats[f] = jnp.zeros((8, COUT), F32)
    stats[f, 0:1] = cell_sum(v) * (1.0 / (v.shape[0] * (W - 2)))
    add_stats(stats, f, v)


def inner_kernel(frames_ref, x_hbm, w_hbm, xc, conv, w_ref, stats, x_ref, x_sems, w_sem):
    first = lax.axis_index("tm") * F
    starts = clip_starts(frames_ref)
    x_copies = [pltpu.make_async_copy(x_hbm.at[f], x_ref.at[f], x_sems.at[f]) for f in range(F)]
    w_copy = pltpu.make_async_copy(w_hbm, w_ref, w_sem)
    for copy in (*x_copies[:2], w_copy, *x_copies[2:]):
        copy.start()
    for f in range(F):
        x_copies[f].wait()
        put_columns(xc, (f,), x_ref[f])
    w_copy.wait()
    for row in (1, 3, 5):
        conv[0, row : row + 2] = inner_taps([xc.at[0]], row, 2, w_ref, (2,))
        frames = [xc.at[source(starts, first, 1, 1)], xc.at[1]]
        conv[1, row : row + 2] = inner_taps(frames, row, 2, w_ref, (1, 2))

    def step(f, carry):
        frames = [xc.at[source(starts, first, f, k)] for k in range(2)] + [xc.at[f]]
        for row in (1, 3, 5):
            out = inner_taps(frames, row, 2, w_ref, (0, 1, 2))
            conv[f, row : row + 2] = out
            (start_stats if row == 1 else add_stats)(stats, f, out)
        return carry

    lax.fori_loop(2, F, step, 0)


def strip_kernel(xc, before, above, below, above_before, below_before, low_out, high_out):
    top, bottom, _, _ = edges()
    for out, at, pick in ((low_out, 0, 0), (high_out, W - 16, 15)):

        def tile(ref, *where):
            return ref[(*where, slice(at, at + 16))].astype(F32)[pick : pick + 1]

        for f in range(F + 2):
            if f < 2:
                rows = [tile(before, f, r) for r in range(H)]
                over, under = tile(above_before, f), tile(below_before, f)
            else:
                g = f - 2
                rows = [
                    xc[g, r, at : at + 16, C : 2 * C].astype(F32)[pick : pick + 1]
                    for r in range(H)
                ]
                over, under = tile(above, g), tile(below, g)
            head = jnp.where(top, rows[0], over)
            tail = jnp.where(bottom, rows[-1], under)
            pad = jnp.zeros((16 - H - 2, C), F32)
            out[f] = jnp.concatenate([head, *rows, tail, pad], axis=0).astype(BF)


def outer_kernel(
    frames_ref,
    w_ref,
    before,
    above,
    below,
    above_before,
    below_before,
    xc,
    conv_in,
    stats_in,
    conv,
    stats,
    early,
    rims,
):
    del conv_in, stats_in
    first = lax.axis_index("tm") * F
    starts = clip_starts(frames_ref)
    top, bottom, _, _ = edges()
    put_columns(early, (0,), before[0])
    put_columns(early, (1,), before[1])
    early[2] = xc[0]
    early[3] = xc[1]
    for f in range(F + 2):
        over, under = (above_before, below_before) if f < 2 else (above, below)
        g = f if f < 2 else f - 2
        own = before.at[f] if f < 2 else xc.at[g, :, :, C : 2 * C]
        rim = jnp.stack([jnp.where(top, own[0], over[g]), jnp.where(bottom, own[H - 1], under[g])])
        put_columns(rims, (f,), rim)

    def outer_rows(f, frame_of):
        parts = []
        for k in range(3):
            s = source(starts, first, f, k)
            frame = frame_of(s)
            upper = [rims[s + 2, 0], frame[0], frame[1]]
            lower = [frame[H - 2], frame[H - 1], rims[s + 2, 1]]
            parts += [jnp.concatenate([u, v], axis=0) for u, v in zip(upper, lower)]
        lhs = jnp.concatenate(parts, axis=1)
        out = jnp.dot(lhs, w_ref[...], preferred_element_type=F32).reshape(2, W, COUT)
        conv[f, 0] = out[0]
        conv[f, H - 1] = out[1]
        return out

    for f, taps in ((0, (0, 1)), (1, (0,))):
        frame_of = lambda s: early.at[s + 2]
        start_stats(stats, f, outer_rows(f, frame_of))
        frames = [frame_of(source(starts, first, f, k)) for k in taps]
        for row in (1, 3, 5):
            out = conv[f, row : row + 2] + inner_taps(frames, row, 2, w_ref, taps)
            conv[f, row : row + 2] = out
            add_stats(stats, f, out)

    def step(f, carry):
        add_stats(stats, f, outer_rows(f, lambda s: xc.at[s]))
        return carry

    lax.fori_loop(2, F, step, 0)


def column_kernel(frames_ref, w_ref, low_ref, high_ref, stats_ref, conv_in, conv, sums):
    del conv_in
    first = lax.axis_index("tm") * F
    starts = clip_starts(frames_ref)
    _, _, left, right = edges()
    total, square = [], []
    pivot = jnp.concatenate([stats_ref[f, 0:1] for f in range(F)], axis=0)
    total = jnp.concatenate([stats_ref[f, 1:2] for f in range(F)], axis=0)
    square = jnp.concatenate([stats_ref[f, 2:3] for f in range(F)], axis=0)
    for ref, edge, dx, at in ((low_ref, left, 0, 0), (high_ref, right, 2, W - 1)):
        lhs = []
        for f in range(F):
            parts = []
            for k in range(3):
                strip = ref[source(starts, first, f, k) + 2].astype(F32)
                strip = jnp.where(edge, 0.0, strip)
                parts += [strip[dy : dy + H] for dy in range(3)]
            lhs.append(jnp.concatenate(parts, axis=1))
        lhs = jnp.concatenate(lhs, axis=0).astype(BF)
        weights = jnp.concatenate(
            [w_ref[(t * 3 + dx) * C : (t * 3 + dx + 1) * C] for t in range(9)], axis=0
        )
        out = jnp.dot(lhs, weights, preferred_element_type=F32)
        added, added_square = [], []
        for f in range(F):
            column = jnp.concatenate([conv[f, r, at : at + 1] for r in range(H)], axis=0)
            column = column + out[f * H : (f + 1) * H]
            for r in range(H):
                conv[f, r, at : at + 1] = column[r : r + 1]
            off = column - pivot[f : f + 1]
            added.append(jnp.sum(off, axis=0, keepdims=True))
            added_square.append(jnp.sum(off * off, axis=0, keepdims=True))
        total = total + jnp.concatenate(added, axis=0)
        square = square + jnp.concatenate(added_square, axis=0)

    cells = float(H * W)
    mean = pivot + total * (1.0 / cells)
    square = square - total * total * (1.0 / cells)
    channel = lax.broadcasted_iota(jnp.int32, (COUT, COUT), 0) // SHARE
    same_group = channel == lax.broadcasted_iota(jnp.int32, (COUT, COUT), 1) // SHARE
    grouped = jnp.dot(mean, same_group.astype(F32), precision=HIGH, preferred_element_type=F32)
    frame_row = lax.broadcasted_iota(jnp.int32, (F, COUT), 0)
    clip = clip_index(starts, first + frame_row)
    clip_sum = clip_count = jnp.zeros((F, COUT), F32)
    for f in range(F):
        same = clip == clip[f : f + 1]
        clip_sum = clip_sum + jnp.where(same, grouped[f : f + 1], 0.0)
        clip_count = clip_count + jnp.where(same, float(SHARE), 0.0)
    centre = clip_sum / clip_count
    off = mean - centre
    square = square + cells * (off * off)
    lane = lax.broadcasted_iota(jnp.int32, (COUT, CLIPS * GROUPS), 1)
    pick = lax.broadcasted_iota(jnp.int32, (COUT, CLIPS * GROUPS), 0) // SHARE == lane % GROUPS
    mine = lax.broadcasted_iota(jnp.int32, (F, CLIPS * GROUPS), 1) // GROUPS
    mine = mine == clip[:, : CLIPS * GROUPS]
    for i, value in enumerate((mean * cells, square)):
        packed = jnp.dot(value, pick.astype(F32), precision=HIGH, preferred_element_type=F32)
        packed = jnp.sum(jnp.where(mine, packed, 0.0), axis=0, keepdims=True)
        sums[:, i * CLIPS * GROUPS : (i + 1) * CLIPS * GROUPS] = packed


def norm_kernel(cells, frames_ref, all_ref, gain, shift, conv, out_ref, held, sems):
    first = lax.axis_index("tm") * F
    starts = clip_starts(frames_ref)
    lanes = CLIPS * GROUPS
    count = all_ref.shape[0]
    value = all_ref[...]
    total, spread = value[:, :lanes], value[:, lanes:]
    which = lax.broadcasted_iota(jnp.int32, (count, lanes), 1) // GROUPS
    begin, length = jnp.zeros_like(which), jnp.zeros_like(which)
    for c in range(CLIPS):
        begin = jnp.where(which == c, starts[c], begin)
        length = jnp.where(which == c, frames_ref[c], length)
    slab = lax.broadcasted_iota(jnp.int32, (count, lanes), 0) // (count // lax.axis_size("tm")) * F
    part = jnp.minimum(slab + F, begin + length) - jnp.maximum(slab, begin)
    part = jnp.maximum(part, 0).astype(F32) * float(H * W * SHARE)
    whole = length[:1].astype(F32) * float(cells * SHARE)
    mean = jnp.sum(total, axis=0, keepdims=True) / whole
    off = total / jnp.maximum(part, 1.0) - mean
    var = jnp.sum(spread + part * (off * off), axis=0, keepdims=True) / whole
    var = var + 1e-06
    scale = lax.rsqrt(var)
    scale = scale * (1.5 - 0.5 * var * scale * scale)

    frame_row = lax.broadcasted_iota(jnp.int32, (F, lanes), 0)
    mine = clip_index(starts, first + frame_row)
    mine = mine == lax.broadcasted_iota(jnp.int32, (F, lanes), 1) // GROUPS
    lane = lax.broadcasted_iota(jnp.int32, (lanes, COUT), 0) % GROUPS
    spreadout = (lane == lax.broadcasted_iota(jnp.int32, (lanes, COUT), 1) // SHARE).astype(F32)

    def per_channel(v):
        v = jnp.where(mine, v, 0.0)
        return jnp.dot(v, spreadout, precision=HIGH, preferred_element_type=F32)

    mean, scale = per_channel(mean), per_channel(scale) * (0.5 * gain[...])
    half = 0.5 * shift[...]

    copies = []
    for f in range(F):

        def row(h, carry):
            u = (conv[f, h] - mean[f : f + 1]) * scale[f : f + 1] + half
            held[f, h] = (u + u * jnp.tanh(u)).astype(BF)
            return carry

        lax.fori_loop(0, H, row, 0)
        copy = pltpu.make_async_copy(held.at[f], out_ref.at[f], sems.at[f])
        copy.start()
        copies.append(copy)
    for copy in copies:
        copy.wait()


def params(mib):
    return pltpu.CompilerParams(vmem_limit_bytes=mib << 20)


def cost(flops, moved):
    return pl.CostEstimate(flops=flops, bytes_accessed=moved, transcendentals=0)


def shards(frames_in, clip_frames, conv_weight, norm_gain, norm_shift):
    n_tm, n_row, n_col = (lax.axis_size(a) for a in ("tm", "row", "col"))
    weights = conv_weight.reshape(27 * C, COUT)
    tail, top_row, bottom_row, tail_top, tail_bottom = pl.pallas_call(
        pack_kernel,
        out_shape=[pltpu.VMEM((2, H, W, C), BF)]
        + [pltpu.VMEM((F, W, C), BF)] * 2
        + [pltpu.VMEM((2, W, C), BF)] * 2,
        in_specs=[HBM],
        out_specs=[VMEM] * 5,
        scratch_shapes=[pltpu.SemaphoreType.DMA((5,))],
        compiler_params=params(8),
        name="pack",
    )(frames_in)
    down = [(i, (i + 1) % n_row) for i in range(n_row)]
    up = [(j, i) for i, j in down]
    later = [(t, (t + 1) % n_tm) for t in range(n_tm)]

    def diagonal(pairs):
        return [(t * n_row + i, u * n_row + j) for t, u in later for i, j in pairs]

    above = lax.ppermute(bottom_row, "row", down)
    below = lax.ppermute(top_row, "row", up)
    before = lax.ppermute(tail, "tm", later)
    above_before = lax.ppermute(tail_bottom, ("tm", "row"), diagonal(down))
    below_before = lax.ppermute(tail_top, ("tm", "row"), diagonal(up))

    conv_shape = pltpu.VMEM((F, H, W, COUT), F32)
    stats_shape = pltpu.VMEM((F, 8, COUT), F32)
    macs = W * 9 * C3 * COUT
    xc, conv, weights, stats = pl.pallas_call(
        inner_kernel,
        out_shape=(
            pltpu.VMEM((F, H, W, C3), BF),
            conv_shape,
            pltpu.VMEM((27 * C, COUT), BF),
            stats_shape,
        ),
        in_specs=[SMEM, HBM, HBM],
        out_specs=[VMEM] * 4,
        scratch_shapes=[
            pltpu.VMEM((F, H, W, C), BF),
            pltpu.SemaphoreType.DMA((F,)),
            pltpu.SemaphoreType.DMA,
        ],
        compiler_params=params(16),
        cost_estimate=cost(2 * 42 * macs, 5 << 20),
        name="inner",
    )(clip_frames, frames_in, weights)
    low, high = pl.pallas_call(
        strip_kernel,
        out_shape=[pltpu.VMEM((F + 2, 16, C), BF)] * 2,
        in_specs=[VMEM] * 6,
        out_specs=[VMEM] * 2,
        compiler_params=params(8),
        cost_estimate=cost(1 << 20, 1 << 16),
        name="strips",
    )(xc, before, above, below, above_before, below_before)
    onward = [(i, (i + 1) % n_col) for i in range(n_col)]
    from_left = lax.ppermute(high, "col", onward)
    from_right = lax.ppermute(low, "col", [(j, i) for i, j in onward])
    conv, stats = pl.pallas_call(
        outer_kernel,
        out_shape=(conv_shape, stats_shape),
        in_specs=[SMEM] + [VMEM] * 9,
        out_specs=[VMEM] * 2,
        input_output_aliases={8: 0, 9: 1},
        scratch_shapes=[
            pltpu.VMEM((4, H, W, C3), BF),
            pltpu.VMEM((F + 2, 2, W, C3), BF),
        ],
        compiler_params=params(18),
        cost_estimate=cost(2 * 22 * macs, 5 << 20),
        name="outer",
    )(clip_frames, weights, before, above, below, above_before, below_before, xc, conv, stats)
    conv, stats = pl.pallas_call(
        column_kernel,
        out_shape=(conv_shape, jax.ShapeDtypeStruct((1, 2 * CLIPS * GROUPS), F32)),
        in_specs=[SMEM] + [VMEM] * 5,
        out_specs=[VMEM] * 2,
        input_output_aliases={5: 0},
        compiler_params=params(12),
        cost_estimate=cost(1 << 27, 1 << 20),
        name="columns",
    )(clip_frames, weights, from_left, from_right, stats, conv)
    count = n_tm * n_row * n_col
    every = jnp.broadcast_to(stats[None], (count, *stats.shape))
    every = lax.all_to_all(every, ("tm", "row", "col"), 0, 0).reshape(count, -1)
    return pl.pallas_call(
        functools.partial(norm_kernel, H * n_row * W * n_col),
        out_shape=jax.ShapeDtypeStruct((F, H, W, COUT), BF),
        in_specs=[SMEM] + [VMEM] * 4,
        out_specs=HBM,
        scratch_shapes=[pltpu.VMEM((F, H, W, COUT), BF), pltpu.SemaphoreType.DMA((F,))],
        compiler_params=params(12),
        cost_estimate=cost(1 << 24, 16 << 20),
        name="norm_silu",
    )(clip_frames, every, norm_gain[None], norm_shift[None], conv)


def solution(mesh):
    return jax.shard_map(
        shards,
        mesh=mesh,
        in_specs=(P("tm", "row", "col", None), P(), P(), P(), P()),
        out_specs=P("tm", "row", "col", None),
        check_vma=False,
    )
```

```python
import functools

import jax
import jax.numpy as jnp
from jax import lax
from jax.experimental import pallas as pl
from jax.experimental.pallas import tpu as pltpu
from jax.sharding import PartitionSpec as P

COUT = 256
GROUPS = 32
CLIPS = 4
SHARE = COUT // GROUPS
F, H, W, C = 8, 8, 160, 128
C3 = 3 * C
BF, F32 = jnp.bfloat16, jnp.float32
VMEM = pl.BlockSpec(memory_space=pltpu.VMEM)
SMEM = pl.BlockSpec(memory_space=pltpu.SMEM)
HBM = pl.BlockSpec(memory_space=pltpu.HBM)


def clip_starts(frames_ref):
    starts = [0]
    for c in range(CLIPS - 1):
        starts.append(starts[-1] + frames_ref[c])
    return starts


def source(starts, first, f, k):
    g = first + f
    start = 0
    for s in starts[1:]:
        start = jnp.where(g >= s, s, start)
    return jnp.maximum(g - 2 + k, start) - first


def clip_index(starts, g):
    c = (g >= starts[1]).astype(jnp.int32)
    for s in starts[2:]:
        c = c + (g >= s).astype(jnp.int32)
    return c


def edges():
    row, col = lax.axis_index("row"), lax.axis_index("col")
    return row == 0, row == lax.axis_size("row") - 1, col == 0, col == lax.axis_size("col") - 1


def put_columns(xc, at, x):
    _, _, left, right = edges()
    low = jnp.where(left, x[:, :1], jnp.zeros_like(x[:, :1]))
    high = jnp.where(right, x[:, -1:], jnp.zeros_like(x[:, -1:]))
    xc[(*at, slice(None), slice(None), slice(0, C))] = jnp.concatenate([low, x[:, :-1]], axis=1)
    xc[(*at, slice(None), slice(None), slice(C, 2 * C))] = x
    xc[(*at, slice(None), slice(None), slice(2 * C, 3 * C))] = jnp.concatenate([x[:, 1:], high], axis=1)


def time_weights(w_ref, taps):
    return w_ref[taps[0] * 3 * C3 : (taps[-1] + 1) * 3 * C3]


def inner_taps(frames, row, rows, w_ref, taps):
    parts = [
        frame[pl.ds(row - 1 + dy, rows)].reshape(rows * W, C3)
        for frame in frames
        for dy in range(3)
    ]
    lhs = jnp.concatenate(parts, axis=1)
    out = jnp.dot(lhs, time_weights(w_ref, taps), preferred_element_type=F32)
    return out.reshape(rows, W, COUT)


def times_zero_one(v, chosen):
    parts = []
    for _ in range(3):
        parts.append(v.astype(BF))
        v = v - parts[-1].astype(F32)
    out = jnp.dot(
        jnp.concatenate(parts, axis=0), chosen.astype(BF), preferred_element_type=F32
    ).reshape(3, v.shape[0], -1)
    return out[0] + (out[1] + out[2])


def cell_sum(v):
    sublane = lax.broadcasted_iota(jnp.int32, (1, 8, COUT), 1)
    v = jnp.concatenate(
        [
            jnp.where(sublane > 0, v[:, :8], 0.0),
            v[:, 8:-8],
            jnp.where(sublane < 7, v[:, -8:], 0.0),
        ],
        axis=1,
    )
    return jnp.sum(v.reshape(-1, COUT), axis=0, keepdims=True)


def add_stats(stats, f, v):
    off = v - stats[f, 0:1]
    stats[f, 1:2] += cell_sum(off)
    stats[f, 2:3] += cell_sum(off * off)


def start_stats(stats, f, v):
    stats[f] = jnp.zeros((8, COUT), F32)
    stats[f, 0:1] = cell_sum(v) * (1.0 / (v.shape[0] * (W - 2)))
    add_stats(stats, f, v)


def load_kernel(
    frames_ref, x_hbm, w_hbm, tail, top_row, bottom_row, tail_top, tail_bottom, xc, w_ref, clips, x_ref, x_sems, w_sem
):
    for c in range(CLIPS):
        clips[c] = frames_ref[c]

    def x_copy(f):
        return pltpu.make_async_copy(x_hbm.at[f], x_ref.at[f], x_sems.at[f])

    for f in range(F):
        x_copy(f).start()
    w_copy = pltpu.make_async_copy(w_hbm, w_ref, w_sem)
    w_copy.start()

    def columns(f, carry):
        x_copy(f).wait()
        top_row[f] = x_ref[f, 0]
        bottom_row[f] = x_ref[f, H - 1]
        put_columns(xc, (f,), x_ref[f])
        return carry

    lax.fori_loop(0, F, columns, 0)
    tail[...] = x_ref[F - 2 :]
    tail_top[...] = x_ref[F - 2 :, 0]
    tail_bottom[...] = x_ref[F - 2 :, H - 1]
    w_copy.wait()


def inner_kernel(frames_ref, xc, w_ref, conv, stats):
    first = lax.axis_index("tm") * F
    starts = clip_starts(frames_ref)

    def first_frames(i, carry):
        row = 1 + 2 * i
        conv[0, pl.ds(row, 2)] = inner_taps([xc.at[0]], row, 2, w_ref, (2,))
        frames = [xc.at[source(starts, first, 1, 1)], xc.at[1]]
        conv[1, pl.ds(row, 2)] = inner_taps(frames, row, 2, w_ref, (1, 2))
        return carry

    lax.fori_loop(0, 3, first_frames, 0, unroll=3)

    def step(i, carry):
        for j in range(3):
            f = 2 + 3 * i + j
            frames = [xc.at[source(starts, first, f, k)] for k in range(2)] + [xc.at[f]]
            for row in (1, 3, 5):
                out = inner_taps(frames, row, 2, w_ref, (0, 1, 2))
                conv[f, row : row + 2] = out
                (start_stats if row == 1 else add_stats)(stats, f, out)
        return carry

    lax.fori_loop(0, (F - 2) // 3, step, 0)


def strip_kernel(xc, before, above, below, above_before, below_before, low_out, high_out):
    top, bottom, _, _ = edges()
    for out, at, pick in ((low_out, 0, 0), (high_out, W - 16, 15)):

        def tile(ref, *where):
            return ref[(*where, slice(at, at + 16))].astype(F32)[pick : pick + 1]

        for f in range(F + 2):
            if f < 2:
                rows = [tile(before, f, r) for r in range(H)]
                over, under = tile(above_before, f), tile(below_before, f)
            else:
                g = f - 2
                rows = [
                    xc[g, r, at : at + 16, C : 2 * C].astype(F32)[pick : pick + 1]
                    for r in range(H)
                ]
                over, under = tile(above, g), tile(below, g)
            head = jnp.where(top, rows[0], over)
            tail = jnp.where(bottom, rows[-1], under)
            pad = jnp.zeros((16 - H - 2, C), F32)
            out[f] = jnp.concatenate([head, *rows, tail, pad], axis=0).astype(BF)


def outer_kernel(
    frames_ref,
    w_ref,
    before,
    above,
    below,
    above_before,
    below_before,
    xc,
    conv_in,
    stats_in,
    conv,
    stats,
    early,
    early_rims,
    rims,
):
    del conv_in, stats_in
    first = lax.axis_index("tm") * F
    starts = clip_starts(frames_ref)
    top, bottom, _, _ = edges()

    def fill_rims(ref, at, own, over, under):
        rim = jnp.stack([jnp.where(top, own[0], over), jnp.where(bottom, own[H - 1], under)])
        put_columns(ref, (at,), rim)

    for f in range(F):
        fill_rims(rims, f, xc.at[f, :, :, C : 2 * C], above[f], below[f])

    def fill_early(i):
        if i == 2:
            for f in range(2):
                early[2 + f] = xc[f]
                early_rims[2 + f] = rims[f]
        else:
            put_columns(early, (i,), before[i])
            fill_rims(early_rims, i, before.at[i], above_before[i], below_before[i])

    def outer_rows(f, place, frames, edge):
        parts = []
        for k in range(3):
            s = source(starts, first, f, k) + place
            frame, rim = frames.at[s], edge.at[s]
            upper = [rim[0], frame[0], frame[1]]
            lower = [frame[H - 2], frame[H - 1], rim[1]]
            parts += [jnp.concatenate([u, v], axis=0) for u, v in zip(upper, lower)]
        lhs = jnp.concatenate(parts, axis=1)
        out = jnp.dot(lhs, w_ref[...], preferred_element_type=F32).reshape(2, W, COUT)
        conv[f, 0] = out[0]
        conv[f, H - 1] = out[1]
        return out

    def step(i, carry):
        for j in range(6):
            f = 2 + 6 * i + j
            add_stats(stats, f, outer_rows(f, 0, xc, rims))
        return carry

    fill_early(0)
    fill_early(1)
    fill_early(2)
    lax.fori_loop(0, (F - 2) // 6, step, 0)
    for f in range(2):
        start_stats(stats, f, outer_rows(f, 2, early, early_rims))

    def first_frames(i, carry):
        row = 1 + 2 * i
        for f, taps in ((0, (0, 1)), (1, (0,))):
            frames = [early.at[source(starts, first, f, k) + 2] for k in taps]
            out = conv[f, pl.ds(row, 2)] + inner_taps(frames, row, 2, w_ref, taps)
            conv[f, pl.ds(row, 2)] = out
            add_stats(stats, f, out)
        return carry

    lax.fori_loop(0, 3, first_frames, 0, unroll=3)


def column_kernel(frames_ref, w_ref, low_ref, high_ref, stats_ref, conv_in, conv, sums):
    del conv_in
    first = lax.axis_index("tm") * F
    starts = clip_starts(frames_ref)
    _, _, left, right = edges()
    total, square = [], []
    pivot = jnp.concatenate([stats_ref[f, 0:1] for f in range(F)], axis=0)
    total = jnp.concatenate([stats_ref[f, 1:2] for f in range(F)], axis=0)
    square = jnp.concatenate([stats_ref[f, 2:3] for f in range(F)], axis=0)
    for ref, edge, dx, at in ((low_ref, left, 0, 0), (high_ref, right, 2, W - 1)):
        lhs = []
        for f in range(F):
            parts = []
            for k in range(3):
                strip = ref[source(starts, first, f, k) + 2].astype(F32)
                strip = jnp.where(edge, 0.0, strip)
                parts += [strip[dy : dy + H] for dy in range(3)]
            lhs.append(jnp.concatenate(parts, axis=1))
        lhs = jnp.concatenate(lhs, axis=0).astype(BF)
        weights = jnp.concatenate(
            [w_ref[(t * 3 + dx) * C : (t * 3 + dx + 1) * C] for t in range(9)], axis=0
        )
        out = jnp.dot(lhs, weights, preferred_element_type=F32)
        added, added_square = [], []
        for f in range(F):
            column = jnp.concatenate([conv[f, r, at : at + 1] for r in range(H)], axis=0)
            column = column + out[f * H : (f + 1) * H]
            for r in range(H):
                conv[f, r, at : at + 1] = column[r : r + 1]
            off = column - pivot[f : f + 1]
            added.append(jnp.sum(off, axis=0, keepdims=True))
            added_square.append(jnp.sum(off * off, axis=0, keepdims=True))
        total = total + jnp.concatenate(added, axis=0)
        square = square + jnp.concatenate(added_square, axis=0)

    cells = float(H * W)
    mean = pivot + total * (1.0 / cells)
    square = square - total * total * (1.0 / cells)
    channel = lax.broadcasted_iota(jnp.int32, (COUT, COUT), 0) // SHARE
    same_group = channel == lax.broadcasted_iota(jnp.int32, (COUT, COUT), 1) // SHARE
    grouped = times_zero_one(mean, same_group)
    frame_row = lax.broadcasted_iota(jnp.int32, (F, COUT), 0)
    clip = clip_index(starts, first + frame_row)
    clip_sum = clip_count = jnp.zeros((F, COUT), F32)
    for f in range(F):
        same = clip == clip[f : f + 1]
        clip_sum = clip_sum + jnp.where(same, grouped[f : f + 1], 0.0)
        clip_count = clip_count + jnp.where(same, float(SHARE), 0.0)
    centre = clip_sum / clip_count
    off = mean - centre
    square = square + cells * (off * off)
    lane = lax.broadcasted_iota(jnp.int32, (COUT, CLIPS * GROUPS), 1)
    pick = lax.broadcasted_iota(jnp.int32, (COUT, CLIPS * GROUPS), 0) // SHARE == lane % GROUPS
    mine = lax.broadcasted_iota(jnp.int32, (F, CLIPS * GROUPS), 1) // GROUPS
    mine = mine == clip[:, : CLIPS * GROUPS]
    packed = times_zero_one(jnp.concatenate([mean * cells, square], axis=0), pick)
    for i in range(2):
        value = jnp.where(mine, packed[i * F : (i + 1) * F], 0.0)
        value = jnp.sum(value, axis=0, keepdims=True)
        sums[:, i * CLIPS * GROUPS : (i + 1) * CLIPS * GROUPS] = value


def norm_kernel(cells, frames_ref, all_ref, gain, shift, conv, out_ref, held, sems, per_frame):
    first = lax.axis_index("tm") * F
    starts = clip_starts(frames_ref)
    lanes = CLIPS * GROUPS
    count = all_ref.shape[0]
    value = all_ref[...]
    total, spread = value[:, :lanes], value[:, lanes:]
    which = lax.broadcasted_iota(jnp.int32, (count, lanes), 1) // GROUPS
    begin, length = jnp.zeros_like(which), jnp.zeros_like(which)
    for c in range(CLIPS):
        begin = jnp.where(which == c, starts[c], begin)
        length = jnp.where(which == c, frames_ref[c], length)
    slab = lax.broadcasted_iota(jnp.int32, (count, lanes), 0) // (count // lax.axis_size("tm")) * F
    part = jnp.minimum(slab + F, begin + length) - jnp.maximum(slab, begin)
    part = jnp.maximum(part, 0).astype(F32) * float(H * W * SHARE)
    whole = length[:1].astype(F32) * float(cells * SHARE)
    mean = jnp.sum(total, axis=0, keepdims=True) / whole
    off = total / jnp.maximum(part, 1.0) - mean
    var = jnp.sum(spread + part * (off * off), axis=0, keepdims=True) / whole
    var = var + 1e-06
    scale = lax.rsqrt(var)
    scale = scale * (1.5 - 0.5 * var * scale * scale)

    frame_row = lax.broadcasted_iota(jnp.int32, (F, lanes), 0)
    mine = clip_index(starts, first + frame_row)
    mine = mine == lax.broadcasted_iota(jnp.int32, (F, lanes), 1) // GROUPS
    lane = lax.broadcasted_iota(jnp.int32, (lanes, COUT), 0) % GROUPS
    chosen = lane == lax.broadcasted_iota(jnp.int32, (lanes, COUT), 1) // SHARE
    both = [jnp.where(mine, v, 0.0) for v in (mean, scale)]
    both = times_zero_one(jnp.concatenate(both, axis=0), chosen)
    mean, scale = both[:F], both[F:] * (0.5 * gain[...])
    half = 0.5 * shift[...]

    def out_copy(f):
        return pltpu.make_async_copy(held.at[f], out_ref.at[f], sems.at[f])

    for f in range(F):
        per_frame[f] = jnp.concatenate([mean[f : f + 1], scale[f : f + 1], half], axis=0)

    def frame(f, carry):
        for h in range(H):
            u = (conv[f, h] - per_frame[f, 0:1]) * per_frame[f, 1:2] + per_frame[f, 2:3]
            held[f, h] = (u + u * jnp.tanh(u)).astype(BF)
        out_copy(f).start()
        return carry

    lax.fori_loop(0, F, frame, 0)
    for f in range(F):
        out_copy(f).wait()


def params(mib):
    return pltpu.CompilerParams(vmem_limit_bytes=mib << 20)


def cost(flops, moved):
    return pl.CostEstimate(flops=flops, bytes_accessed=moved, transcendentals=0)


def shards(frames_in, clip_frames, conv_weight, norm_gain, norm_shift):
    n_tm, n_row, n_col = (lax.axis_size(a) for a in ("tm", "row", "col"))
    weights = conv_weight.reshape(27 * C, COUT)
    tail, top_row, bottom_row, tail_top, tail_bottom, xc, weights, clips = pl.pallas_call(
        load_kernel,
        out_shape=[pltpu.VMEM((2, H, W, C), BF)]
        + [pltpu.VMEM((F, W, C), BF)] * 2
        + [pltpu.VMEM((2, W, C), BF)] * 2
        + [pltpu.VMEM((F, H, W, C3), BF), pltpu.VMEM((27 * C, COUT), BF)]
        + [pltpu.SMEM((CLIPS,), jnp.int32)],
        in_specs=[SMEM] + [HBM] * 2,
        out_specs=[VMEM] * 7 + [SMEM],
        scratch_shapes=[
            pltpu.VMEM((F, H, W, C), BF),
            pltpu.SemaphoreType.DMA((F,)),
            pltpu.SemaphoreType.DMA,
        ],
        compiler_params=params(52),
        name="load",
    )(clip_frames, frames_in, weights)
    down = [(i, (i + 1) % n_row) for i in range(n_row)]
    up = [(j, i) for i, j in down]
    later = [(t, (t + 1) % n_tm) for t in range(n_tm)]

    def diagonal(pairs):
        return [(t * n_row + i, u * n_row + j) for t, u in later for i, j in pairs]

    above = lax.ppermute(bottom_row, "row", down)
    below = lax.ppermute(top_row, "row", up)
    before = lax.ppermute(tail, "tm", later)
    above_before = lax.ppermute(tail_bottom, ("tm", "row"), diagonal(down))
    below_before = lax.ppermute(tail_top, ("tm", "row"), diagonal(up))

    conv_shape = pltpu.VMEM((F, H, W, COUT), F32)
    stats_shape = pltpu.VMEM((F, 8, COUT), F32)
    macs = W * 9 * C3 * COUT
    conv, stats = pl.pallas_call(
        inner_kernel,
        out_shape=(conv_shape, stats_shape),
        in_specs=[SMEM, VMEM, VMEM],
        out_specs=[VMEM] * 2,
        compiler_params=params(12),
        cost_estimate=cost(2 * 42 * macs, 5 << 20),
        name="inner",
    )(clips, xc, weights)
    low, high = pl.pallas_call(
        strip_kernel,
        out_shape=[pltpu.VMEM((F + 2, 16, C), BF)] * 2,
        in_specs=[VMEM] * 6,
        out_specs=[VMEM] * 2,
        compiler_params=params(8),
        cost_estimate=cost(1 << 20, 1 << 16),
        name="strips",
    )(xc, before, above, below, above_before, below_before)
    onward = [(i, (i + 1) % n_col) for i in range(n_col)]
    from_left = lax.ppermute(high, "col", onward)
    from_right = lax.ppermute(low, "col", [(j, i) for i, j in onward])
    conv, stats = pl.pallas_call(
        outer_kernel,
        out_shape=(conv_shape, stats_shape),
        in_specs=[SMEM] + [VMEM] * 9,
        out_specs=[VMEM] * 2,
        input_output_aliases={8: 0, 9: 1},
        scratch_shapes=[
            pltpu.VMEM((4, H, W, C3), BF),
            pltpu.VMEM((4, 2, W, C3), BF),
            pltpu.VMEM((F, 2, W, C3), BF),
        ],
        compiler_params=params(18),
        cost_estimate=cost(2 * 22 * macs, 5 << 20),
        name="outer",
    )(clip_frames, weights, before, above, below, above_before, below_before, xc, conv, stats)
    conv, stats = pl.pallas_call(
        column_kernel,
        out_shape=(conv_shape, jax.ShapeDtypeStruct((1, 2 * CLIPS * GROUPS), F32)),
        in_specs=[SMEM] + [VMEM] * 5,
        out_specs=[VMEM] * 2,
        input_output_aliases={5: 0},
        compiler_params=params(12),
        cost_estimate=cost(1 << 27, 1 << 20),
        name="columns",
    )(clip_frames, weights, from_left, from_right, stats, conv)
    count = n_tm * n_row * n_col
    every = jnp.broadcast_to(stats[None], (count, *stats.shape))
    every = lax.all_to_all(every, ("tm", "row", "col"), 0, 0).reshape(count, -1)
    return pl.pallas_call(
        functools.partial(norm_kernel, H * n_row * W * n_col),
        out_shape=jax.ShapeDtypeStruct((F, H, W, COUT), BF),
        in_specs=[SMEM] + [VMEM] * 4,
        out_specs=HBM,
        scratch_shapes=[
            pltpu.VMEM((F, H, W, COUT), BF),
            pltpu.SemaphoreType.DMA((F,)),
            pltpu.VMEM((F, 3, COUT), F32),
        ],
        compiler_params=params(12),
        cost_estimate=cost(1 << 24, 16 << 20),
        name="norm_silu",
    )(clip_frames, every, norm_gain[None], norm_shift[None], conv)


def solution(mesh):
    return jax.shard_map(
        shards,
        mesh=mesh,
        in_specs=(P("tm", "row", "col", None), P(), P(), P(), P()),
        out_specs=P("tm", "row", "col", None),
        check_vma=False,
    )
```

```python
import functools

import jax
import jax.numpy as jnp
from jax import lax
from jax.experimental import pallas as pl
from jax.experimental.pallas import tpu as pltpu
from jax.sharding import PartitionSpec as P

COUT = 256
GROUPS = 32
CLIPS = 4
SHARE = COUT // GROUPS
F, H, W, C = 8, 8, 160, 128
C3 = 3 * C
LATE = 6
BF, F32 = jnp.bfloat16, jnp.float32
VMEM = pl.BlockSpec(memory_space=pltpu.VMEM)
SMEM = pl.BlockSpec(memory_space=pltpu.SMEM)
HBM = pl.BlockSpec(memory_space=pltpu.HBM)


def clip_starts(frames_ref):
    starts = [0]
    for c in range(CLIPS - 1):
        starts.append(starts[-1] + frames_ref[c])
    return starts


def source(starts, first, f, k):
    g = first + f
    start = 0
    for s in starts[1:]:
        start = jnp.where(g >= s, s, start)
    return jnp.maximum(g - 2 + k, start) - first


def clip_index(starts, g):
    c = (g >= starts[1]).astype(jnp.int32)
    for s in starts[2:]:
        c = c + (g >= s).astype(jnp.int32)
    return c


def edges():
    row, col = lax.axis_index("row"), lax.axis_index("col")
    return row == 0, row == lax.axis_size("row") - 1, col == 0, col == lax.axis_size("col") - 1


def put_columns(xc, at, x):
    _, _, left, right = edges()
    low = jnp.where(left, x[:, :1], jnp.zeros_like(x[:, :1]))
    high = jnp.where(right, x[:, -1:], jnp.zeros_like(x[:, -1:]))
    xc[(*at, slice(None), slice(None), slice(0, C))] = jnp.concatenate([low, x[:, :-1]], axis=1)
    xc[(*at, slice(None), slice(None), slice(C, 2 * C))] = x
    xc[(*at, slice(None), slice(None), slice(2 * C, 3 * C))] = jnp.concatenate([x[:, 1:], high], axis=1)


def time_weights(w_ref, taps):
    return w_ref[taps[0] * 3 * C3 : (taps[-1] + 1) * 3 * C3]


def inner_taps(frames, row, rows, w_ref, taps):
    parts = [
        frame[pl.ds(row - 1 + dy, rows)].reshape(rows * W, C3)
        for frame in frames
        for dy in range(3)
    ]
    lhs = jnp.concatenate(parts, axis=1)
    out = jnp.dot(lhs, time_weights(w_ref, taps), preferred_element_type=F32)
    return out.reshape(rows, W, COUT)


def times_zero_one(v, chosen):
    parts = []
    for _ in range(3):
        parts.append(v.astype(BF))
        v = v - parts[-1].astype(F32)
    out = jnp.dot(
        jnp.concatenate(parts, axis=0), chosen.astype(BF), preferred_element_type=F32
    ).reshape(3, v.shape[0], -1)
    return out[0] + (out[1] + out[2])


def cell_sum(v):
    sublane = lax.broadcasted_iota(jnp.int32, (1, 8, COUT), 1)
    v = jnp.concatenate(
        [
            jnp.where(sublane > 0, v[:, :8], 0.0),
            v[:, 8:-8],
            jnp.where(sublane < 7, v[:, -8:], 0.0),
        ],
        axis=1,
    )
    return jnp.sum(v.reshape(-1, COUT), axis=0, keepdims=True)


def add_stats(stats, f, v):
    off = v - stats[f, 0:1]
    stats[f, 1:2] += cell_sum(off)
    stats[f, 2:3] += cell_sum(off * off)


def start_stats(stats, f, v):
    stats[f] = jnp.zeros((8, COUT), F32)
    stats[f, 0:1] = cell_sum(v) * (1.0 / (v.shape[0] * (W - 2)))
    add_stats(stats, f, v)


def load_kernel(
    frames_hbm, x_hbm, w_hbm, tail, top_row, bottom_row, tail_top, tail_bottom, xc, w_ref, clips, x_ref, x_sems, w_sem, c_sem
):
    c_copy = pltpu.make_async_copy(frames_hbm, clips, c_sem)
    c_copy.start()

    def x_copy(f):
        return pltpu.make_async_copy(x_hbm.at[f], x_ref.at[f], x_sems.at[f])

    for f in range(F):
        x_copy(f).start()
    w_copy = pltpu.make_async_copy(w_hbm, w_ref, w_sem)
    w_copy.start()

    def columns(f, carry):
        x_copy(f).wait()
        top_row[f] = x_ref[f, 0]
        bottom_row[f] = x_ref[f, H - 1]
        put_columns(xc, (f,), x_ref[f])
        return carry

    lax.fori_loop(0, F, columns, 0)
    tail[...] = x_ref[F - 2 :]
    tail_top[...] = x_ref[F - 2 :, 0]
    tail_bottom[...] = x_ref[F - 2 :, H - 1]
    w_copy.wait()
    c_copy.wait()


def inner_frame(f, first, starts, xc, w_ref, conv, stats):
    frames = [xc.at[source(starts, first, f, k)] for k in range(2)] + [xc.at[f]]
    for row in (1, 3, 5):
        out = inner_taps(frames, row, 2, w_ref, (0, 1, 2))
        conv[f, row : row + 2] = out
        (start_stats if row == 1 else add_stats)(stats, f, out)


def inner_kernel(frames_ref, xc, w_ref, conv, stats):
    first = lax.axis_index("tm") * F
    starts = clip_starts(frames_ref)

    def first_frames(i, carry):
        row = 1 + 2 * i
        conv[0, pl.ds(row, 2)] = inner_taps([xc.at[0]], row, 2, w_ref, (2,))
        frames = [xc.at[source(starts, first, 1, 1)], xc.at[1]]
        conv[1, pl.ds(row, 2)] = inner_taps(frames, row, 2, w_ref, (1, 2))
        return carry

    lax.fori_loop(0, 3, first_frames, 0, unroll=3)

    for f in range(2, LATE):
        inner_frame(f, first, starts, xc, w_ref, conv, stats)


def strip_kernel(xc, before, above, below, above_before, below_before, low_out, high_out):
    top, bottom, _, _ = edges()
    for out, at, pick in ((low_out, 0, 0), (high_out, W - 16, 15)):

        def tile(ref, *where):
            return ref[(*where, slice(at, at + 16))].astype(F32)[pick : pick + 1]

        for f in range(F + 2):
            if f < 2:
                rows = [tile(before, f, r) for r in range(H)]
                over, under = tile(above_before, f), tile(below_before, f)
            else:
                g = f - 2
                rows = [
                    xc[g, r, at : at + 16, C : 2 * C].astype(F32)[pick : pick + 1]
                    for r in range(H)
                ]
                over, under = tile(above, g), tile(below, g)
            head = jnp.where(top, rows[0], over)
            tail = jnp.where(bottom, rows[-1], under)
            pad = jnp.zeros((16 - H - 2, C), F32)
            out[f] = jnp.concatenate([head, *rows, tail, pad], axis=0).astype(BF)


def outer_kernel(
    frames_ref,
    w_ref,
    before,
    above,
    below,
    above_before,
    below_before,
    xc,
    conv_in,
    stats_in,
    conv,
    stats,
    early,
    early_rims,
    rims,
):
    del conv_in, stats_in
    first = lax.axis_index("tm") * F
    starts = clip_starts(frames_ref)
    top, bottom, _, _ = edges()

    def fill_rims(ref, at, own, over, under):
        rim = jnp.stack([jnp.where(top, own[0], over), jnp.where(bottom, own[H - 1], under)])
        put_columns(ref, (at,), rim)

    def fill_early(i):
        if i == 2:
            for f in range(2):
                early[2 + f] = xc[f]
                early_rims[2 + f] = rims[f]
        else:
            put_columns(early, (i,), before[i])
            fill_rims(early_rims, i, before.at[i], above_before[i], below_before[i])

    def outer_rows(f, place, frames, edge):
        parts = []
        for k in range(3):
            s = source(starts, first, f, k) + place
            frame, rim = frames.at[s], edge.at[s]
            upper = [rim[0], frame[0], frame[1]]
            lower = [frame[H - 2], frame[H - 1], rim[1]]
            parts += [jnp.concatenate([u, v], axis=0) for u, v in zip(upper, lower)]
        lhs = jnp.concatenate(parts, axis=1)
        out = jnp.dot(lhs, w_ref[...], preferred_element_type=F32).reshape(2, W, COUT)
        conv[f, 0] = out[0]
        conv[f, H - 1] = out[1]
        return out

    for f in range(LATE, F):
        for g in range(f - LATE, F, F - LATE):
            fill_rims(rims, g, xc.at[g, :, :, C : 2 * C], above[g], below[g])
        if f == F - 1:
            for i in range(3):
                fill_early(i)
        inner_frame(f, first, starts, xc, w_ref, conv, stats)
    for f in range(2, F):
        add_stats(stats, f, outer_rows(f, 0, xc, rims))
    for f in range(2):
        start_stats(stats, f, outer_rows(f, 2, early, early_rims))

    def first_frames(i, carry):
        row = 1 + 2 * i
        for f, taps in ((0, (0, 1)), (1, (0,))):
            frames = [early.at[source(starts, first, f, k) + 2] for k in taps]
            out = conv[f, pl.ds(row, 2)] + inner_taps(frames, row, 2, w_ref, taps)
            conv[f, pl.ds(row, 2)] = out
            add_stats(stats, f, out)
        return carry

    lax.fori_loop(0, 3, first_frames, 0, unroll=3)


def column_kernel(frames_ref, w_ref, low_ref, high_ref, stats_ref, conv_in, conv, sums):
    del conv_in
    first = lax.axis_index("tm") * F
    starts = clip_starts(frames_ref)
    _, _, left, right = edges()
    total, square = [], []
    pivot = jnp.concatenate([stats_ref[f, 0:1] for f in range(F)], axis=0)
    total = jnp.concatenate([stats_ref[f, 1:2] for f in range(F)], axis=0)
    square = jnp.concatenate([stats_ref[f, 2:3] for f in range(F)], axis=0)
    for ref, edge, dx, at in ((low_ref, left, 0, 0), (high_ref, right, 2, W - 1)):
        lhs = []
        for f in range(F):
            parts = []
            for k in range(3):
                strip = ref[source(starts, first, f, k) + 2].astype(F32)
                strip = jnp.where(edge, 0.0, strip)
                parts += [strip[dy : dy + H] for dy in range(3)]
            lhs.append(jnp.concatenate(parts, axis=1))
        lhs = jnp.concatenate(lhs, axis=0).astype(BF)
        weights = jnp.concatenate(
            [w_ref[(t * 3 + dx) * C : (t * 3 + dx + 1) * C] for t in range(9)], axis=0
        )
        out = jnp.dot(lhs, weights, preferred_element_type=F32)
        added, added_square = [], []
        for f in range(F):
            column = jnp.concatenate([conv[f, r, at : at + 1] for r in range(H)], axis=0)
            column = column + out[f * H : (f + 1) * H]
            for r in range(H):
                conv[f, r, at : at + 1] = column[r : r + 1]
            off = column - pivot[f : f + 1]
            added.append(jnp.sum(off, axis=0, keepdims=True))
            added_square.append(jnp.sum(off * off, axis=0, keepdims=True))
        total = total + jnp.concatenate(added, axis=0)
        square = square + jnp.concatenate(added_square, axis=0)

    cells = float(H * W)
    mean = pivot + total * (1.0 / cells)
    square = square - total * total * (1.0 / cells)
    channel = lax.broadcasted_iota(jnp.int32, (COUT, COUT), 0) // SHARE
    same_group = channel == lax.broadcasted_iota(jnp.int32, (COUT, COUT), 1) // SHARE
    grouped = times_zero_one(mean, same_group)
    frame_row = lax.broadcasted_iota(jnp.int32, (F, COUT), 0)
    clip = clip_index(starts, first + frame_row)
    clip_sum = clip_count = jnp.zeros((F, COUT), F32)
    for f in range(F):
        same = clip == clip[f : f + 1]
        clip_sum = clip_sum + jnp.where(same, grouped[f : f + 1], 0.0)
        clip_count = clip_count + jnp.where(same, float(SHARE), 0.0)
    centre = clip_sum / clip_count
    off = mean - centre
    square = square + cells * (off * off)
    lane = lax.broadcasted_iota(jnp.int32, (COUT, CLIPS * GROUPS), 1)
    pick = lax.broadcasted_iota(jnp.int32, (COUT, CLIPS * GROUPS), 0) // SHARE == lane % GROUPS
    mine = lax.broadcasted_iota(jnp.int32, (F, CLIPS * GROUPS), 1) // GROUPS
    mine = mine == clip[:, : CLIPS * GROUPS]
    packed = times_zero_one(jnp.concatenate([mean * cells, square], axis=0), pick)
    for i in range(2):
        value = jnp.where(mine, packed[i * F : (i + 1) * F], 0.0)
        value = jnp.sum(value, axis=0, keepdims=True)
        sums[:, i * CLIPS * GROUPS : (i + 1) * CLIPS * GROUPS] = value


def norm_kernel(cells, frames_ref, all_ref, gain, shift, conv, out_ref, held, sems, per_frame):
    first = lax.axis_index("tm") * F
    starts = clip_starts(frames_ref)
    lanes = CLIPS * GROUPS
    count = all_ref.shape[0]
    value = all_ref[...]
    total, spread = value[:, :lanes], value[:, lanes:]
    which = lax.broadcasted_iota(jnp.int32, (count, lanes), 1) // GROUPS
    begin, length = jnp.zeros_like(which), jnp.zeros_like(which)
    for c in range(CLIPS):
        begin = jnp.where(which == c, starts[c], begin)
        length = jnp.where(which == c, frames_ref[c], length)
    slab = lax.broadcasted_iota(jnp.int32, (count, lanes), 0) // (count // lax.axis_size("tm")) * F
    part = jnp.minimum(slab + F, begin + length) - jnp.maximum(slab, begin)
    part = jnp.maximum(part, 0).astype(F32) * float(H * W * SHARE)
    whole = length[:1].astype(F32) * float(cells * SHARE)
    mean = jnp.sum(total, axis=0, keepdims=True) / whole
    off = total / jnp.maximum(part, 1.0) - mean
    var = jnp.sum(spread + part * (off * off), axis=0, keepdims=True) / whole
    var = var + 1e-06
    scale = lax.rsqrt(var)
    scale = scale * (1.5 - 0.5 * var * scale * scale)

    frame_row = lax.broadcasted_iota(jnp.int32, (F, lanes), 0)
    mine = clip_index(starts, first + frame_row)
    mine = mine == lax.broadcasted_iota(jnp.int32, (F, lanes), 1) // GROUPS
    lane = lax.broadcasted_iota(jnp.int32, (lanes, COUT), 0) % GROUPS
    chosen = lane == lax.broadcasted_iota(jnp.int32, (lanes, COUT), 1) // SHARE
    both = [jnp.where(mine, v, 0.0) for v in (mean, scale)]
    both = times_zero_one(jnp.concatenate(both, axis=0), chosen)
    mean, scale = both[:F], both[F:] * (0.5 * gain[...])
    offset = 0.5 * shift[...] - mean * scale

    def out_copy(f):
        return pltpu.make_async_copy(held.at[f], out_ref.at[f], sems.at[f])

    for f in range(F):
        per_frame[f] = jnp.concatenate([scale[f : f + 1], offset[f : f + 1]], axis=0)

    def frame(f, carry):
        for h in range(H):
            u = conv[f, h] * per_frame[f, 0:1] + per_frame[f, 1:2]
            held[f, h] = (u + u * jnp.tanh(u)).astype(BF)
        out_copy(f).start()
        return carry

    lax.fori_loop(0, F, frame, 0)
    for f in range(F):
        out_copy(f).wait()


def params(mib):
    return pltpu.CompilerParams(vmem_limit_bytes=mib << 20)


def cost(flops, moved):
    return pl.CostEstimate(flops=flops, bytes_accessed=moved, transcendentals=0)


def shards(frames_in, clip_frames, conv_weight, norm_gain, norm_shift):
    n_tm, n_row, n_col = (lax.axis_size(a) for a in ("tm", "row", "col"))
    weights = conv_weight.reshape(27 * C, COUT)
    tail, top_row, bottom_row, tail_top, tail_bottom, xc, weights, clips = pl.pallas_call(
        load_kernel,
        out_shape=[pltpu.VMEM((2, H, W, C), BF)]
        + [pltpu.VMEM((F, W, C), BF)] * 2
        + [pltpu.VMEM((2, W, C), BF)] * 2
        + [pltpu.VMEM((F, H, W, C3), BF), pltpu.VMEM((27 * C, COUT), BF)]
        + [pltpu.SMEM((CLIPS,), jnp.int32)],
        in_specs=[HBM] * 3,
        out_specs=[VMEM] * 7 + [SMEM],
        scratch_shapes=[
            pltpu.VMEM((F, H, W, C), BF),
            pltpu.SemaphoreType.DMA((F,)),
            pltpu.SemaphoreType.DMA,
            pltpu.SemaphoreType.DMA,
        ],
        compiler_params=params(52),
        name="load",
    )(clip_frames, frames_in, weights)
    down = [(i, (i + 1) % n_row) for i in range(n_row)]
    up = [(j, i) for i, j in down]
    later = [(t, (t + 1) % n_tm) for t in range(n_tm)]

    def diagonal(pairs):
        return [(t * n_row + i, u * n_row + j) for t, u in later for i, j in pairs]

    above = lax.ppermute(bottom_row, "row", down)
    below = lax.ppermute(top_row, "row", up)
    before = lax.ppermute(tail, "tm", later)
    above_before = lax.ppermute(tail_bottom, ("tm", "row"), diagonal(down))
    below_before = lax.ppermute(tail_top, ("tm", "row"), diagonal(up))

    conv_shape = pltpu.VMEM((F, H, W, COUT), F32)
    stats_shape = pltpu.VMEM((F, 8, COUT), F32)
    macs = W * 9 * C3 * COUT
    conv, stats = pl.pallas_call(
        inner_kernel,
        out_shape=(conv_shape, stats_shape),
        in_specs=[SMEM, VMEM, VMEM],
        out_specs=[VMEM] * 2,
        compiler_params=params(12),
        cost_estimate=cost(2 * 42 * macs, 5 << 20),
        name="inner",
    )(clips, xc, weights)
    low, high = pl.pallas_call(
        strip_kernel,
        out_shape=[pltpu.VMEM((F + 2, 16, C), BF)] * 2,
        in_specs=[VMEM] * 6,
        out_specs=[VMEM] * 2,
        compiler_params=params(8),
        cost_estimate=cost(1 << 20, 1 << 16),
        name="strips",
    )(xc, before, above, below, above_before, below_before)
    onward = [(i, (i + 1) % n_col) for i in range(n_col)]
    from_left = lax.ppermute(high, "col", onward)
    from_right = lax.ppermute(low, "col", [(j, i) for i, j in onward])
    conv, stats = pl.pallas_call(
        outer_kernel,
        out_shape=(conv_shape, stats_shape),
        in_specs=[SMEM] + [VMEM] * 9,
        out_specs=[VMEM] * 2,
        input_output_aliases={8: 0, 9: 1},
        scratch_shapes=[
            pltpu.VMEM((4, H, W, C3), BF),
            pltpu.VMEM((4, 2, W, C3), BF),
            pltpu.VMEM((F, 2, W, C3), BF),
        ],
        compiler_params=params(18),
        cost_estimate=cost(2 * 22 * macs, 5 << 20),
        name="outer",
    )(clip_frames, weights, before, above, below, above_before, below_before, xc, conv, stats)
    conv, stats = pl.pallas_call(
        column_kernel,
        out_shape=(conv_shape, jax.ShapeDtypeStruct((1, 2 * CLIPS * GROUPS), F32)),
        in_specs=[SMEM] + [VMEM] * 5,
        out_specs=[VMEM] * 2,
        input_output_aliases={5: 0},
        compiler_params=params(12),
        cost_estimate=cost(1 << 27, 1 << 20),
        name="columns",
    )(clip_frames, weights, from_left, from_right, stats, conv)
    count = n_tm * n_row * n_col
    every = jnp.broadcast_to(stats[None], (count, *stats.shape))
    every = lax.all_to_all(every, ("tm", "row", "col"), 0, 0).reshape(count, -1)
    return pl.pallas_call(
        functools.partial(norm_kernel, H * n_row * W * n_col),
        out_shape=jax.ShapeDtypeStruct((F, H, W, COUT), BF),
        in_specs=[SMEM] + [VMEM] * 4,
        out_specs=HBM,
        scratch_shapes=[
            pltpu.VMEM((F, H, W, COUT), BF),
            pltpu.SemaphoreType.DMA((F,)),
            pltpu.VMEM((F, 2, COUT), F32),
        ],
        compiler_params=params(12),
        cost_estimate=cost(1 << 24, 16 << 20),
        name="norm_silu",
    )(clip_frames, every, norm_gain[None], norm_shift[None], conv)


def solution(mesh):
    return jax.shard_map(
        shards,
        mesh=mesh,
        in_specs=(P("tm", "row", "col", None), P(), P(), P(), P()),
        out_specs=P("tm", "row", "col", None),
        check_vma=False,
    )
```

```python
import functools

import jax
import jax.numpy as jnp
from jax import lax
from jax.experimental import pallas as pl
from jax.experimental.pallas import tpu as pltpu
from jax.sharding import PartitionSpec as P

COUT = 256
GROUPS = 32
CLIPS = 4
SHARE = COUT // GROUPS
F, H, W, C = 8, 8, 160, 128
C3 = 3 * C
BF, F32 = jnp.bfloat16, jnp.float32
VMEM = pl.BlockSpec(memory_space=pltpu.VMEM)
SMEM = pl.BlockSpec(memory_space=pltpu.SMEM)
HBM = pl.BlockSpec(memory_space=pltpu.HBM)


def clip_starts(frames_ref):
    starts = [0]
    for c in range(CLIPS - 1):
        starts.append(starts[-1] + frames_ref[c])
    return starts


def source(starts, first, f, k):
    g = first + f
    start = 0
    for s in starts[1:]:
        start = jnp.where(g >= s, s, start)
    return jnp.maximum(g - 2 + k, start) - first


def clip_index(starts, g):
    c = (g >= starts[1]).astype(jnp.int32)
    for s in starts[2:]:
        c = c + (g >= s).astype(jnp.int32)
    return c


def edges():
    row, col = lax.axis_index("row"), lax.axis_index("col")
    return row == 0, row == lax.axis_size("row") - 1, col == 0, col == lax.axis_size("col") - 1


def put_columns(xc, at, x):
    _, _, left, right = edges()
    low = jnp.where(left, x[:, :1], jnp.zeros_like(x[:, :1]))
    high = jnp.where(right, x[:, -1:], jnp.zeros_like(x[:, -1:]))
    xc[(*at, slice(None), slice(None), slice(0, C))] = jnp.concatenate([low, x[:, :-1]], axis=1)
    xc[(*at, slice(None), slice(None), slice(C, 2 * C))] = x
    xc[(*at, slice(None), slice(None), slice(2 * C, 3 * C))] = jnp.concatenate([x[:, 1:], high], axis=1)


def time_weights(w_ref, taps):
    return w_ref[taps[0] * 3 * C3 : (taps[-1] + 1) * 3 * C3]


def inner_taps(frames, row, rows, w_ref, taps):
    parts = [
        frame[pl.ds(row - 1 + dy, rows)].reshape(rows * W, C3)
        for frame in frames
        for dy in range(3)
    ]
    lhs = jnp.concatenate(parts, axis=1)
    out = jnp.dot(lhs, time_weights(w_ref, taps), preferred_element_type=F32)
    return out.reshape(rows, W, COUT)


def times_zero_one(v, chosen):
    parts = []
    for _ in range(3):
        parts.append(v.astype(BF))
        v = v - parts[-1].astype(F32)
    out = jnp.dot(
        jnp.concatenate(parts, axis=0), chosen.astype(BF), preferred_element_type=F32
    ).reshape(3, v.shape[0], -1)
    return out[0] + (out[1] + out[2])


def cell_sum(v):
    sublane = lax.broadcasted_iota(jnp.int32, (1, 8, COUT), 1)
    v = jnp.concatenate(
        [
            jnp.where(sublane > 0, v[:, :8], 0.0),
            v[:, 8:-8],
            jnp.where(sublane < 7, v[:, -8:], 0.0),
        ],
        axis=1,
    )
    return jnp.sum(v.reshape(-1, COUT), axis=0, keepdims=True)


def add_stats(stats, f, v):
    off = v - stats[f, 0:1]
    stats[f, 1:2] += cell_sum(off)
    stats[f, 2:3] += cell_sum(off * off)


def start_stats(stats, f, v):
    stats[f] = jnp.zeros((8, COUT), F32)
    stats[f, 0:1] = cell_sum(v) * (1.0 / (v.shape[0] * (W - 2)))
    add_stats(stats, f, v)


def load_kernel(
    frames_hbm, x_hbm, w_hbm, tail, top_row, bottom_row, tail_top, tail_bottom, xc, w_ref, clips, x_ref, x_sems, w_sem, c_sem
):
    c_copy = pltpu.make_async_copy(frames_hbm, clips, c_sem)
    c_copy.start()

    def x_copy(f):
        return pltpu.make_async_copy(x_hbm.at[f], x_ref.at[f], x_sems.at[f])

    for f in range(F):
        x_copy(f).start()
    w_copy = pltpu.make_async_copy(w_hbm, w_ref, w_sem)
    w_copy.start()

    def columns(f, carry):
        x_copy(f).wait()
        top_row[f] = x_ref[f, 0]
        bottom_row[f] = x_ref[f, H - 1]
        put_columns(xc, (f,), x_ref[f])
        return carry

    lax.fori_loop(0, F, columns, 0)
    tail[...] = x_ref[F - 2 :]
    tail_top[...] = x_ref[F - 2 :, 0]
    tail_bottom[...] = x_ref[F - 2 :, H - 1]
    w_copy.wait()
    c_copy.wait()


def inner_frame(f, first, starts, xc, w_ref, conv, stats):
    frames = [xc.at[source(starts, first, f, k)] for k in range(2)] + [xc.at[f]]
    for row in (1, 3, 5):
        out = inner_taps(frames, row, 2, w_ref, (0, 1, 2))
        conv[f, row : row + 2] = out
        (start_stats if row == 1 else add_stats)(stats, f, out)


def inner_kernel(frames, opening, frames_ref, xc, w_ref, *refs):
    conv, stats = refs[:2] if opening else refs[-3:-1]
    first = lax.axis_index("tm") * F
    starts = clip_starts(frames_ref)
    for f in frames:
        inner_frame(f, first, starts, xc, w_ref, conv, stats)
    if opening:
        for row in (1, 3, 5):
            conv[0, row : row + 2] = inner_taps([xc.at[0]], row, 2, w_ref, (2,))
            own = [xc.at[source(starts, first, 1, 1)], xc.at[1]]
            conv[1, row : row + 2] = inner_taps(own, row, 2, w_ref, (1, 2))


def inner_part(frames, opening, clips, xc, weights, conv, stats, passed):
    out_shape = [pltpu.VMEM((F, H, W, COUT), F32), pltpu.VMEM((F, 8, COUT), F32)]
    held = [] if opening else [conv, stats, passed]
    if not opening:
        out_shape.append(pltpu.VMEM(passed.shape, passed.dtype))
    count = 3 * len(frames) + 3 * opening
    return pl.pallas_call(
        functools.partial(inner_kernel, frames, opening),
        out_shape=out_shape,
        in_specs=[SMEM] + [VMEM] * (2 + len(held)),
        out_specs=[VMEM] * len(out_shape),
        input_output_aliases={3 + i: i for i in range(len(held))},
        compiler_params=params(12),
        cost_estimate=cost(2 * count * 2 * W * 9 * C3 * COUT, 5 << 20),
        name="inner",
    )(clips, xc, weights, *held)


def strip_kernel(xc, before, above, below, above_before, below_before, low_out, high_out):
    top, bottom, _, _ = edges()
    for out, at, pick in ((low_out, 0, 0), (high_out, W - 16, 15)):

        def tile(ref, *where):
            return ref[(*where, slice(at, at + 16))].astype(F32)[pick : pick + 1]

        for f in range(F + 2):
            if f < 2:
                rows = [tile(before, f, r) for r in range(H)]
                over, under = tile(above_before, f), tile(below_before, f)
            else:
                g = f - 2
                rows = [
                    xc[g, r, at : at + 16, C : 2 * C].astype(F32)[pick : pick + 1]
                    for r in range(H)
                ]
                over, under = tile(above, g), tile(below, g)
            head = jnp.where(top, rows[0], over)
            tail = jnp.where(bottom, rows[-1], under)
            pad = jnp.zeros((16 - H - 2, C), F32)
            out[f] = jnp.concatenate([head, *rows, tail, pad], axis=0).astype(BF)


def outer_kernel(
    frames_ref,
    w_ref,
    before,
    above,
    below,
    above_before,
    below_before,
    xc,
    arrived,
    conv_in,
    stats_in,
    conv,
    stats,
    early,
    early_rims,
    rims,
):
    del arrived, conv_in, stats_in
    first = lax.axis_index("tm") * F
    starts = clip_starts(frames_ref)
    top, bottom, _, _ = edges()

    def fill_rims(ref, at, own, over, under):
        rim = jnp.stack([jnp.where(top, own[0], over), jnp.where(bottom, own[H - 1], under)])
        put_columns(ref, (at,), rim)

    def fill_early(i):
        if i == 2:
            for f in range(2):
                early[2 + f] = xc[f]
                early_rims[2 + f] = rims[f]
        else:
            put_columns(early, (i,), before[i])
            fill_rims(early_rims, i, before.at[i], above_before[i], below_before[i])

    def outer_rows(f, place, frames, edge):
        parts = []
        for k in range(3):
            s = source(starts, first, f, k) + place
            frame, rim = frames.at[s], edge.at[s]
            upper = [rim[0], frame[0], frame[1]]
            lower = [frame[H - 2], frame[H - 1], rim[1]]
            parts += [jnp.concatenate([u, v], axis=0) for u, v in zip(upper, lower)]
        lhs = jnp.concatenate(parts, axis=1)
        out = jnp.dot(lhs, w_ref[...], preferred_element_type=F32).reshape(2, W, COUT)
        conv[f, 0] = out[0]
        conv[f, H - 1] = out[1]
        return out

    for f in range(F):
        fill_rims(rims, f, xc.at[f, :, :, C : 2 * C], above[f], below[f])
    for i in range(3):
        fill_early(i)
    for f in range(2, F):
        add_stats(stats, f, outer_rows(f, 0, xc, rims))
    for f in range(2):
        start_stats(stats, f, outer_rows(f, 2, early, early_rims))

    def first_frames(i, carry):
        row = 1 + 2 * i
        for f, taps in ((0, (0, 1)), (1, (0,))):
            frames = [early.at[source(starts, first, f, k) + 2] for k in taps]
            out = conv[f, pl.ds(row, 2)] + inner_taps(frames, row, 2, w_ref, taps)
            conv[f, pl.ds(row, 2)] = out
            add_stats(stats, f, out)
        return carry

    lax.fori_loop(0, 3, first_frames, 0, unroll=3)


def column_kernel(frames_ref, w_ref, low_ref, high_ref, stats_ref, conv_in, conv, sums):
    del conv_in
    first = lax.axis_index("tm") * F
    starts = clip_starts(frames_ref)
    _, _, left, right = edges()
    total, square = [], []
    pivot = jnp.concatenate([stats_ref[f, 0:1] for f in range(F)], axis=0)
    total = jnp.concatenate([stats_ref[f, 1:2] for f in range(F)], axis=0)
    square = jnp.concatenate([stats_ref[f, 2:3] for f in range(F)], axis=0)
    for ref, edge, dx, at in ((low_ref, left, 0, 0), (high_ref, right, 2, W - 1)):
        lhs = []
        for f in range(F):
            parts = []
            for k in range(3):
                strip = ref[source(starts, first, f, k) + 2].astype(F32)
                strip = jnp.where(edge, 0.0, strip)
                parts += [strip[dy : dy + H] for dy in range(3)]
            lhs.append(jnp.concatenate(parts, axis=1))
        lhs = jnp.concatenate(lhs, axis=0).astype(BF)
        weights = jnp.concatenate(
            [w_ref[(t * 3 + dx) * C : (t * 3 + dx + 1) * C] for t in range(9)], axis=0
        )
        out = jnp.dot(lhs, weights, preferred_element_type=F32)
        added, added_square = [], []
        for f in range(F):
            column = jnp.concatenate([conv[f, r, at : at + 1] for r in range(H)], axis=0)
            column = column + out[f * H : (f + 1) * H]
            for r in range(H):
                conv[f, r, at : at + 1] = column[r : r + 1]
            off = column - pivot[f : f + 1]
            added.append(jnp.sum(off, axis=0, keepdims=True))
            added_square.append(jnp.sum(off * off, axis=0, keepdims=True))
        total = total + jnp.concatenate(added, axis=0)
        square = square + jnp.concatenate(added_square, axis=0)

    cells = float(H * W)
    mean = pivot + total * (1.0 / cells)
    square = square - total * total * (1.0 / cells)
    channel = lax.broadcasted_iota(jnp.int32, (COUT, COUT), 0) // SHARE
    same_group = channel == lax.broadcasted_iota(jnp.int32, (COUT, COUT), 1) // SHARE
    grouped = times_zero_one(mean, same_group)
    frame_row = lax.broadcasted_iota(jnp.int32, (F, COUT), 0)
    clip = clip_index(starts, first + frame_row)
    clip_sum = clip_count = jnp.zeros((F, COUT), F32)
    for f in range(F):
        same = clip == clip[f : f + 1]
        clip_sum = clip_sum + jnp.where(same, grouped[f : f + 1], 0.0)
        clip_count = clip_count + jnp.where(same, float(SHARE), 0.0)
    centre = clip_sum / clip_count
    off = mean - centre
    square = square + cells * (off * off)
    lane = lax.broadcasted_iota(jnp.int32, (COUT, CLIPS * GROUPS), 1)
    pick = lax.broadcasted_iota(jnp.int32, (COUT, CLIPS * GROUPS), 0) // SHARE == lane % GROUPS
    mine = lax.broadcasted_iota(jnp.int32, (F, CLIPS * GROUPS), 1) // GROUPS
    mine = mine == clip[:, : CLIPS * GROUPS]
    packed = times_zero_one(jnp.concatenate([mean * cells, square], axis=0), pick)
    for i in range(2):
        value = jnp.where(mine, packed[i * F : (i + 1) * F], 0.0)
        value = jnp.sum(value, axis=0, keepdims=True)
        sums[:, i * CLIPS * GROUPS : (i + 1) * CLIPS * GROUPS] = value


def norm_kernel(cells, frames_ref, all_ref, gain, shift, conv, out_ref, held, sems, per_frame):
    first = lax.axis_index("tm") * F
    starts = clip_starts(frames_ref)
    lanes = CLIPS * GROUPS
    count = all_ref.shape[0]
    value = all_ref[...]
    total, spread = value[:, :lanes], value[:, lanes:]
    which = lax.broadcasted_iota(jnp.int32, (count, lanes), 1) // GROUPS
    begin, length = jnp.zeros_like(which), jnp.zeros_like(which)
    for c in range(CLIPS):
        begin = jnp.where(which == c, starts[c], begin)
        length = jnp.where(which == c, frames_ref[c], length)
    slab = lax.broadcasted_iota(jnp.int32, (count, lanes), 0) // (count // lax.axis_size("tm")) * F
    part = jnp.minimum(slab + F, begin + length) - jnp.maximum(slab, begin)
    part = jnp.maximum(part, 0).astype(F32) * float(H * W * SHARE)
    whole = length[:1].astype(F32) * float(cells * SHARE)
    mean = jnp.sum(total, axis=0, keepdims=True) / whole
    off = total / jnp.maximum(part, 1.0) - mean
    var = jnp.sum(spread + part * (off * off), axis=0, keepdims=True) / whole
    var = var + 1e-06
    scale = lax.rsqrt(var)
    scale = scale * (1.5 - 0.5 * var * scale * scale)

    frame_row = lax.broadcasted_iota(jnp.int32, (F, lanes), 0)
    mine = clip_index(starts, first + frame_row)
    mine = mine == lax.broadcasted_iota(jnp.int32, (F, lanes), 1) // GROUPS
    lane = lax.broadcasted_iota(jnp.int32, (lanes, COUT), 0) % GROUPS
    chosen = lane == lax.broadcasted_iota(jnp.int32, (lanes, COUT), 1) // SHARE
    both = [jnp.where(mine, v, 0.0) for v in (mean, scale)]
    both = times_zero_one(jnp.concatenate(both, axis=0), chosen)
    mean, scale = both[:F], both[F:] * (0.5 * gain[...])
    offset = 0.5 * shift[...] - mean * scale

    def out_copy(f):
        f, h = f // 2, f % 2 * (H // 2)
        rows = (f, pl.ds(h, H // 2))
        return pltpu.make_async_copy(held.at[rows], out_ref.at[rows], sems.at[2 * f + h // (H // 2)])

    for f in range(F):
        per_frame[f] = jnp.concatenate([scale[f : f + 1], offset[f : f + 1]], axis=0)

    def half_frame(i, carry):
        f = i // 2
        for r in range(H // 2):
            h = i % 2 * (H // 2) + r
            u = conv[f, h] * per_frame[f, 0:1] + per_frame[f, 1:2]
            held[f, h] = (u + u * jnp.tanh(u)).astype(BF)
        out_copy(i).start()
        return carry

    lax.fori_loop(0, 2 * F, half_frame, 0)
    for i in range(2 * F):
        out_copy(i).wait()


def params(mib):
    return pltpu.CompilerParams(vmem_limit_bytes=mib << 20)


def cost(flops, moved):
    return pl.CostEstimate(flops=flops, bytes_accessed=moved, transcendentals=0)


def shards(frames_in, clip_frames, conv_weight, norm_gain, norm_shift):
    n_tm, n_row, n_col = (lax.axis_size(a) for a in ("tm", "row", "col"))
    weights = conv_weight.reshape(27 * C, COUT)
    tail, top_row, bottom_row, tail_top, tail_bottom, xc, weights, clips = pl.pallas_call(
        load_kernel,
        out_shape=[pltpu.VMEM((2, H, W, C), BF)]
        + [pltpu.VMEM((F, W, C), BF)] * 2
        + [pltpu.VMEM((2, W, C), BF)] * 2
        + [pltpu.VMEM((F, H, W, C3), BF), pltpu.VMEM((27 * C, COUT), BF)]
        + [pltpu.SMEM((CLIPS,), jnp.int32)],
        in_specs=[HBM] * 3,
        out_specs=[VMEM] * 7 + [SMEM],
        scratch_shapes=[
            pltpu.VMEM((F, H, W, C), BF),
            pltpu.SemaphoreType.DMA((F,)),
            pltpu.SemaphoreType.DMA,
            pltpu.SemaphoreType.DMA,
        ],
        compiler_params=params(52),
        name="load",
    )(clip_frames, frames_in, weights)
    down = [(i, (i + 1) % n_row) for i in range(n_row)]
    up = [(j, i) for i, j in down]
    later = [(t, (t + 1) % n_tm) for t in range(n_tm)]

    def diagonal(pairs):
        return [(t * n_row + i, u * n_row + j) for t, u in later for i, j in pairs]

    conv_shape = pltpu.VMEM((F, H, W, COUT), F32)
    stats_shape = pltpu.VMEM((F, 8, COUT), F32)
    macs = W * 9 * C3 * COUT
    part = lambda *args: inner_part(args[0], args[1], clips, xc, weights, *args[2:])
    above = lax.ppermute(bottom_row, "row", down)
    below = lax.ppermute(top_row, "row", up)
    before = lax.ppermute(tail, "tm", later)
    above_before = lax.ppermute(tail_bottom, ("tm", "row"), diagonal(down))
    below_before = lax.ppermute(tail_top, ("tm", "row"), diagonal(up))
    conv, stats = part((2, 3, 4, 5, 6), True, None, None, None)
    low, high = pl.pallas_call(
        strip_kernel,
        out_shape=[pltpu.VMEM((F + 2, 16, C), BF)] * 2,
        in_specs=[VMEM] * 6,
        out_specs=[VMEM] * 2,
        compiler_params=params(8),
        cost_estimate=cost(1 << 20, 1 << 16),
        name="strips",
    )(xc, before, above, below, above_before, below_before)
    onward = [(i, (i + 1) % n_col) for i in range(n_col)]
    from_left = lax.ppermute(high, "col", onward)
    conv, stats, low = part((7,), False, conv, stats, low)
    from_right = lax.ppermute(low, "col", [(j, i) for i, j in onward])
    conv, stats = pl.pallas_call(
        outer_kernel,
        out_shape=(conv_shape, stats_shape),
        in_specs=[SMEM] + [VMEM] * 10,
        out_specs=[VMEM] * 2,
        input_output_aliases={9: 0, 10: 1},
        scratch_shapes=[
            pltpu.VMEM((4, H, W, C3), BF),
            pltpu.VMEM((4, 2, W, C3), BF),
            pltpu.VMEM((F, 2, W, C3), BF),
        ],
        compiler_params=params(18),
        cost_estimate=cost(2 * 22 * macs, 5 << 20),
        name="outer",
    )(clips, weights, before, above, below, above_before, below_before, xc, from_left, conv, stats)
    conv, stats = pl.pallas_call(
        column_kernel,
        out_shape=(conv_shape, jax.ShapeDtypeStruct((1, 2 * CLIPS * GROUPS), F32)),
        in_specs=[SMEM] + [VMEM] * 5,
        out_specs=[VMEM] * 2,
        input_output_aliases={5: 0},
        compiler_params=params(12),
        cost_estimate=cost(1 << 27, 1 << 20),
        name="columns",
    )(clips, weights, from_left, from_right, stats, conv)
    count = n_tm * n_row * n_col
    every = jnp.broadcast_to(stats[None], (count, *stats.shape))
    every = lax.all_to_all(every, ("tm", "row", "col"), 0, 0).reshape(count, -1)
    return pl.pallas_call(
        functools.partial(norm_kernel, H * n_row * W * n_col),
        out_shape=jax.ShapeDtypeStruct((F, H, W, COUT), BF),
        in_specs=[SMEM] + [VMEM] * 4,
        out_specs=HBM,
        scratch_shapes=[
            pltpu.VMEM((F, H, W, COUT), BF),
            pltpu.SemaphoreType.DMA((2 * F,)),
            pltpu.VMEM((F, 2, COUT), F32),
        ],
        compiler_params=params(12),
        cost_estimate=cost(1 << 24, 16 << 20),
        name="norm_silu",
    )(clips, every, norm_gain[None], norm_shift[None], conv)


def solution(mesh):
    return jax.shard_map(
        shards,
        mesh=mesh,
        in_specs=(P("tm", "row", "col", None), P(), P(), P(), P()),
        out_specs=P("tm", "row", "col", None),
        check_vma=False,
    )
```

```python
import functools

import jax
import jax.numpy as jnp
from jax import lax
from jax.experimental import pallas as pl
from jax.experimental.pallas import tpu as pltpu
from jax.sharding import PartitionSpec as P

COUT = 256
GROUPS = 32
CLIPS = 4
SHARE = COUT // GROUPS
F, H, W, C = 8, 8, 160, 128
C3 = 3 * C
BF, F32 = jnp.bfloat16, jnp.float32
VMEM = pl.BlockSpec(memory_space=pltpu.VMEM)
SMEM = pl.BlockSpec(memory_space=pltpu.SMEM)
HBM = pl.BlockSpec(memory_space=pltpu.HBM)


def clip_starts(frames_ref):
    starts = [0]
    for c in range(CLIPS - 1):
        starts.append(starts[-1] + frames_ref[c])
    return starts


def source(starts, first, f, k):
    g = first + f
    start = 0
    for s in starts[1:]:
        start = jnp.where(g >= s, s, start)
    return jnp.maximum(g - 2 + k, start) - first


def clip_index(starts, g):
    c = (g >= starts[1]).astype(jnp.int32)
    for s in starts[2:]:
        c = c + (g >= s).astype(jnp.int32)
    return c


def edges():
    row, col = lax.axis_index("row"), lax.axis_index("col")
    return row == 0, row == lax.axis_size("row") - 1, col == 0, col == lax.axis_size("col") - 1


def put_columns(xc, at, x, middle=True):
    _, _, left, right = edges()
    low = jnp.where(left, x[:, :1], jnp.zeros_like(x[:, :1]))
    high = jnp.where(right, x[:, -1:], jnp.zeros_like(x[:, -1:]))
    xc[(*at, slice(None), slice(None), slice(0, C))] = jnp.concatenate([low, x[:, :-1]], axis=1)
    if middle:
        xc[(*at, slice(None), slice(None), slice(C, 2 * C))] = x
    xc[(*at, slice(None), slice(None), slice(2 * C, 3 * C))] = jnp.concatenate([x[:, 1:], high], axis=1)


def time_weights(w_ref, taps):
    return w_ref[taps[0] * 3 * C3 : (taps[-1] + 1) * 3 * C3]


def inner_taps(frames, row, rows, w_ref, taps):
    parts = [
        frame[pl.ds(row - 1 + dy, rows)].reshape(rows * W, C3)
        for frame in frames
        for dy in range(3)
    ]
    lhs = jnp.concatenate(parts, axis=1)
    out = jnp.dot(lhs, time_weights(w_ref, taps), preferred_element_type=F32)
    return out.reshape(rows, W, COUT)


def times_zero_one(v, chosen):
    parts = []
    for _ in range(3):
        parts.append(v.astype(BF))
        v = v - parts[-1].astype(F32)
    out = jnp.dot(
        jnp.concatenate(parts, axis=0), chosen.astype(BF), preferred_element_type=F32
    ).reshape(3, v.shape[0], -1)
    return out[0] + (out[1] + out[2])


def cell_sum(v):
    sublane = lax.broadcasted_iota(jnp.int32, (1, 8, COUT), 1)
    v = jnp.concatenate(
        [
            jnp.where(sublane > 0, v[:, :8], 0.0),
            v[:, 8:-8],
            jnp.where(sublane < 7, v[:, -8:], 0.0),
        ],
        axis=1,
    )
    return jnp.sum(v.reshape(-1, COUT), axis=0, keepdims=True)


def add_stats(stats, f, v):
    off = v - stats[f, 0:1]
    stats[f, 1:2] += cell_sum(off)
    stats[f, 2:3] += cell_sum(off * off)


def start_stats(stats, f, v):
    stats[f] = jnp.zeros((8, COUT), F32)
    stats[f, 0:1] = cell_sum(v) * (1.0 / (v.shape[0] * (W - 2)))
    add_stats(stats, f, v)


def load_kernel(
    frames_hbm,
    x_hbm,
    w_hbm,
    tail,
    top_row,
    bottom_row,
    tail_top,
    tail_bottom,
    xc,
    w_ref,
    clips,
    x_sems,
    w_sem,
    c_sem,
):
    c_copy = pltpu.make_async_copy(frames_hbm, clips, c_sem)
    c_copy.start()

    own = xc.at[:, :, :, C : 2 * C]

    def x_copy(f):
        return pltpu.make_async_copy(x_hbm.at[f], own.at[f], x_sems.at[f])

    for f in range(F):
        x_copy(f).start()
    w_copy = pltpu.make_async_copy(w_hbm, w_ref, w_sem)
    w_copy.start()

    def columns(f, carry):
        x_copy(f).wait()
        top_row[f] = own[f, 0]
        bottom_row[f] = own[f, H - 1]
        put_columns(xc, (f,), own[f], middle=False)
        return carry

    lax.fori_loop(0, F, columns, 0)
    tail[...] = own[F - 2 :]
    tail_top[...] = own[F - 2 :, 0]
    tail_bottom[...] = own[F - 2 :, H - 1]
    w_copy.wait()
    c_copy.wait()


def inner_frame(f, first, starts, xc, w_ref, conv, stats):
    frames = [xc.at[source(starts, first, f, k)] for k in range(2)] + [xc.at[f]]
    for row in (1, 3, 5):
        out = inner_taps(frames, row, 2, w_ref, (0, 1, 2))
        conv[f, row : row + 2] = out
        (start_stats if row == 1 else add_stats)(stats, f, out)


def inner_kernel(frames, opening, frames_ref, xc, w_ref, *refs):
    conv, stats = refs[:2] if opening else refs[-3:-1]
    first = lax.axis_index("tm") * F
    starts = clip_starts(frames_ref)
    for f in frames:
        inner_frame(f, first, starts, xc, w_ref, conv, stats)
    if opening:
        for row in (1, 3, 5):
            conv[0, row : row + 2] = inner_taps([xc.at[0]], row, 2, w_ref, (2,))
            own = [xc.at[source(starts, first, 1, 1)], xc.at[1]]
            conv[1, row : row + 2] = inner_taps(own, row, 2, w_ref, (1, 2))


def inner_part(frames, opening, clips, xc, weights, conv, stats, passed):
    out_shape = [pltpu.VMEM((F, H, W, COUT), F32), pltpu.VMEM((F, 8, COUT), F32)]
    held = [] if opening else [conv, stats, passed]
    if not opening:
        out_shape.append(pltpu.VMEM(passed.shape, passed.dtype))
    count = 3 * len(frames) + 3 * opening
    return pl.pallas_call(
        functools.partial(inner_kernel, frames, opening),
        out_shape=out_shape,
        in_specs=[SMEM] + [VMEM] * (2 + len(held)),
        out_specs=[VMEM] * len(out_shape),
        input_output_aliases={3 + i: i for i in range(len(held))},
        compiler_params=params(12),
        cost_estimate=cost(2 * count * 2 * W * 9 * C3 * COUT, 5 << 20),
        name="inner",
    )(clips, xc, weights, *held)


def strip_kernel(xc, before, above, below, above_before, below_before, low_out, high_out):
    top, bottom, _, _ = edges()
    for out, at, pick in ((low_out, 0, 0), (high_out, W - 16, 15)):

        def tile(ref, *where):
            return ref[(*where, slice(at, at + 16))].astype(F32)[pick : pick + 1]

        for f in range(F + 2):
            if f < 2:
                rows = [tile(before, f, r) for r in range(H)]
                over, under = tile(above_before, f), tile(below_before, f)
            else:
                g = f - 2
                rows = [
                    xc[g, r, at : at + 16, C : 2 * C].astype(F32)[pick : pick + 1]
                    for r in range(H)
                ]
                over, under = tile(above, g), tile(below, g)
            head = jnp.where(top, rows[0], over)
            tail = jnp.where(bottom, rows[-1], under)
            pad = jnp.zeros((16 - H - 2, C), F32)
            out[f] = jnp.concatenate([head, *rows, tail, pad], axis=0).astype(BF)


def outer_kernel(
    frames_ref,
    w_ref,
    before,
    above,
    below,
    above_before,
    below_before,
    xc,
    arrived,
    conv_in,
    stats_in,
    conv,
    stats,
    early,
    early_rims,
    rims,
):
    del arrived, conv_in, stats_in
    first = lax.axis_index("tm") * F
    starts = clip_starts(frames_ref)
    top, bottom, _, _ = edges()

    def fill_rims(ref, at, own, over, under):
        rim = jnp.stack([jnp.where(top, own[0], over), jnp.where(bottom, own[H - 1], under)])
        put_columns(ref, (at,), rim)

    def fill_early(i):
        if i == 2:
            for f in range(2):
                early[2 + f] = xc[f]
                early_rims[2 + f] = rims[f]
        else:
            put_columns(early, (i,), before[i])
            fill_rims(early_rims, i, before.at[i], above_before[i], below_before[i])

    def outer_rows(f, place, frames, edge):
        parts = []
        for k in range(3):
            s = source(starts, first, f, k) + place
            frame, rim = frames.at[s], edge.at[s]
            upper = [rim[0], frame[0], frame[1]]
            lower = [frame[H - 2], frame[H - 1], rim[1]]
            parts += [jnp.concatenate([u, v], axis=0) for u, v in zip(upper, lower)]
        lhs = jnp.concatenate(parts, axis=1)
        out = jnp.dot(lhs, w_ref[...], preferred_element_type=F32).reshape(2, W, COUT)
        conv[f, 0] = out[0]
        conv[f, H - 1] = out[1]
        return out

    for f in range(F):
        fill_rims(rims, f, xc.at[f, :, :, C : 2 * C], above[f], below[f])
    for i in range(3):
        fill_early(i)
    for f in range(2, F):
        add_stats(stats, f, outer_rows(f, 0, xc, rims))
    for f in range(2):
        start_stats(stats, f, outer_rows(f, 2, early, early_rims))

    def first_frames(i, carry):
        row = 1 + 2 * i
        for f, taps in ((0, (0, 1)), (1, (0,))):
            frames = [early.at[source(starts, first, f, k) + 2] for k in taps]
            out = conv[f, pl.ds(row, 2)] + inner_taps(frames, row, 2, w_ref, taps)
            conv[f, pl.ds(row, 2)] = out
            add_stats(stats, f, out)
        return carry

    lax.fori_loop(0, 3, first_frames, 0, unroll=3)


def column_kernel(frames_ref, w_ref, low_ref, high_ref, stats_ref, conv_in, conv, sums):
    del conv_in
    first = lax.axis_index("tm") * F
    starts = clip_starts(frames_ref)
    _, _, left, right = edges()
    total, square = [], []
    pivot = jnp.concatenate([stats_ref[f, 0:1] for f in range(F)], axis=0)
    total = jnp.concatenate([stats_ref[f, 1:2] for f in range(F)], axis=0)
    square = jnp.concatenate([stats_ref[f, 2:3] for f in range(F)], axis=0)
    for ref, edge, dx, at in ((low_ref, left, 0, 0), (high_ref, right, 2, W - 1)):
        lhs = []
        for f in range(F):
            parts = []
            for k in range(3):
                strip = ref[source(starts, first, f, k) + 2].astype(F32)
                strip = jnp.where(edge, 0.0, strip)
                parts += [strip[dy : dy + H] for dy in range(3)]
            lhs.append(jnp.concatenate(parts, axis=1))
        lhs = jnp.concatenate(lhs, axis=0).astype(BF)
        weights = jnp.concatenate(
            [w_ref[(t * 3 + dx) * C : (t * 3 + dx + 1) * C] for t in range(9)], axis=0
        )
        out = jnp.dot(lhs, weights, preferred_element_type=F32)
        added, added_square = [], []
        for f in range(F):
            column = jnp.concatenate([conv[f, r, at : at + 1] for r in range(H)], axis=0)
            column = column + out[f * H : (f + 1) * H]
            for r in range(H):
                conv[f, r, at : at + 1] = column[r : r + 1]
            off = column - pivot[f : f + 1]
            added.append(jnp.sum(off, axis=0, keepdims=True))
            added_square.append(jnp.sum(off * off, axis=0, keepdims=True))
        total = total + jnp.concatenate(added, axis=0)
        square = square + jnp.concatenate(added_square, axis=0)

    cells = float(H * W)
    mean = pivot + total * (1.0 / cells)
    square = square - total * total * (1.0 / cells)
    channel = lax.broadcasted_iota(jnp.int32, (COUT, COUT), 0) // SHARE
    same_group = channel == lax.broadcasted_iota(jnp.int32, (COUT, COUT), 1) // SHARE
    grouped = times_zero_one(mean, same_group)
    frame_row = lax.broadcasted_iota(jnp.int32, (F, COUT), 0)
    clip = clip_index(starts, first + frame_row)
    clip_sum = clip_count = jnp.zeros((F, COUT), F32)
    for f in range(F):
        same = clip == clip[f : f + 1]
        clip_sum = clip_sum + jnp.where(same, grouped[f : f + 1], 0.0)
        clip_count = clip_count + jnp.where(same, float(SHARE), 0.0)
    centre = clip_sum / clip_count
    off = mean - centre
    square = square + cells * (off * off)
    lane = lax.broadcasted_iota(jnp.int32, (COUT, CLIPS * GROUPS), 1)
    pick = lax.broadcasted_iota(jnp.int32, (COUT, CLIPS * GROUPS), 0) // SHARE == lane % GROUPS
    mine = lax.broadcasted_iota(jnp.int32, (F, CLIPS * GROUPS), 1) // GROUPS
    mine = mine == clip[:, : CLIPS * GROUPS]
    packed = times_zero_one(jnp.concatenate([mean * cells, square], axis=0), pick)
    for i in range(2):
        value = jnp.where(mine, packed[i * F : (i + 1) * F], 0.0)
        value = jnp.sum(value, axis=0, keepdims=True)
        sums[:, i * CLIPS * GROUPS : (i + 1) * CLIPS * GROUPS] = value


def norm_kernel(cells, frames_ref, all_ref, gain, shift, conv, out_ref, held, sems, per_frame):
    first = lax.axis_index("tm") * F
    starts = clip_starts(frames_ref)
    lanes = CLIPS * GROUPS
    count = all_ref.shape[0]
    value = all_ref[...]
    total, spread = value[:, :lanes], value[:, lanes:]
    which = lax.broadcasted_iota(jnp.int32, (count, lanes), 1) // GROUPS
    begin, length = jnp.zeros_like(which), jnp.zeros_like(which)
    for c in range(CLIPS):
        begin = jnp.where(which == c, starts[c], begin)
        length = jnp.where(which == c, frames_ref[c], length)
    slab = lax.broadcasted_iota(jnp.int32, (count, lanes), 0) // (count // lax.axis_size("tm")) * F
    part = jnp.minimum(slab + F, begin + length) - jnp.maximum(slab, begin)
    part = jnp.maximum(part, 0).astype(F32) * float(H * W * SHARE)
    whole = length[:1].astype(F32) * float(cells * SHARE)
    mean = jnp.sum(total, axis=0, keepdims=True) / whole
    off = total / jnp.maximum(part, 1.0) - mean
    var = jnp.sum(spread + part * (off * off), axis=0, keepdims=True) / whole
    var = var + 1e-06
    scale = lax.rsqrt(var)
    scale = scale * (1.5 - 0.5 * var * scale * scale)

    frame_row = lax.broadcasted_iota(jnp.int32, (F, lanes), 0)
    mine = clip_index(starts, first + frame_row)
    mine = mine == lax.broadcasted_iota(jnp.int32, (F, lanes), 1) // GROUPS
    lane = lax.broadcasted_iota(jnp.int32, (lanes, COUT), 0) % GROUPS
    chosen = lane == lax.broadcasted_iota(jnp.int32, (lanes, COUT), 1) // SHARE
    both = [jnp.where(mine, v, 0.0) for v in (mean, scale)]
    both = times_zero_one(jnp.concatenate(both, axis=0), chosen)
    mean, scale = both[:F], both[F:] * (0.5 * gain[...])
    offset = 0.5 * shift[...] - mean * scale

    def out_copy(f):
        f, h = f // 2, f % 2 * (H // 2)
        rows = (f, pl.ds(h, H // 2))
        return pltpu.make_async_copy(held.at[rows], out_ref.at[rows], sems.at[2 * f + h // (H // 2)])

    for f in range(F):
        per_frame[f] = jnp.concatenate([scale[f : f + 1], offset[f : f + 1]], axis=0)

    def half_frame(i, carry):
        f = i // 2
        for r in range(H // 2):
            h = i % 2 * (H // 2) + r
            u = conv[f, h] * per_frame[f, 0:1] + per_frame[f, 1:2]
            held[f, h] = (u + u * jnp.tanh(u)).astype(BF)
        out_copy(i).start()
        return carry

    lax.fori_loop(0, 2 * F, half_frame, 0)
    for i in range(2 * F):
        out_copy(i).wait()


def params(mib):
    return pltpu.CompilerParams(vmem_limit_bytes=mib << 20)


def cost(flops, moved):
    return pl.CostEstimate(flops=flops, bytes_accessed=moved, transcendentals=0)


def shards(frames_in, clip_frames, conv_weight, norm_gain, norm_shift):
    n_tm, n_row, n_col = (lax.axis_size(a) for a in ("tm", "row", "col"))
    weights = conv_weight.reshape(27 * C, COUT)
    tail, top_row, bottom_row, tail_top, tail_bottom, xc, weights, clips = pl.pallas_call(
        load_kernel,
        out_shape=[pltpu.VMEM((2, H, W, C), BF)]
        + [pltpu.VMEM((F, W, C), BF)] * 2
        + [pltpu.VMEM((2, W, C), BF)] * 2
        + [pltpu.VMEM((F, H, W, C3), BF), pltpu.VMEM((27 * C, COUT), BF)]
        + [pltpu.SMEM((CLIPS,), jnp.int32)],
        in_specs=[HBM] * 3,
        out_specs=[VMEM] * 7 + [SMEM],
        scratch_shapes=[
            pltpu.SemaphoreType.DMA((F,)),
            pltpu.SemaphoreType.DMA,
            pltpu.SemaphoreType.DMA,
        ],
        compiler_params=params(52),
        name="load",
    )(clip_frames, frames_in, weights)
    down = [(i, (i + 1) % n_row) for i in range(n_row)]
    up = [(j, i) for i, j in down]
    later = [(t, (t + 1) % n_tm) for t in range(n_tm)]

    def diagonal(pairs):
        return [(t * n_row + i, u * n_row + j) for t, u in later for i, j in pairs]

    conv_shape = pltpu.VMEM((F, H, W, COUT), F32)
    stats_shape = pltpu.VMEM((F, 8, COUT), F32)
    macs = W * 9 * C3 * COUT
    part = lambda *args: inner_part(args[0], args[1], clips, xc, weights, *args[2:])
    above = lax.ppermute(bottom_row, "row", down)
    below = lax.ppermute(top_row, "row", up)
    before = lax.ppermute(tail, "tm", later)
    above_before = lax.ppermute(tail_bottom, ("tm", "row"), diagonal(down))
    below_before = lax.ppermute(tail_top, ("tm", "row"), diagonal(up))
    conv, stats = part((2, 3, 4, 5, 6), True, None, None, None)
    low, high = pl.pallas_call(
        strip_kernel,
        out_shape=[pltpu.VMEM((F + 2, 16, C), BF)] * 2,
        in_specs=[VMEM] * 6,
        out_specs=[VMEM] * 2,
        compiler_params=params(8),
        cost_estimate=cost(1 << 20, 1 << 16),
        name="strips",
    )(xc, before, above, below, above_before, below_before)
    onward = [(i, (i + 1) % n_col) for i in range(n_col)]
    from_left = lax.ppermute(high, "col", onward)
    conv, stats, low = part((7,), False, conv, stats, low)
    from_right = lax.ppermute(low, "col", [(j, i) for i, j in onward])
    conv, stats = pl.pallas_call(
        outer_kernel,
        out_shape=(conv_shape, stats_shape),
        in_specs=[SMEM] + [VMEM] * 10,
        out_specs=[VMEM] * 2,
        input_output_aliases={9: 0, 10: 1},
        scratch_shapes=[
            pltpu.VMEM((4, H, W, C3), BF),
            pltpu.VMEM((4, 2, W, C3), BF),
            pltpu.VMEM((F, 2, W, C3), BF),
        ],
        compiler_params=params(18),
        cost_estimate=cost(2 * 22 * macs, 5 << 20),
        name="outer",
    )(clips, weights, before, above, below, above_before, below_before, xc, from_left, conv, stats)
    conv, stats = pl.pallas_call(
        column_kernel,
        out_shape=(conv_shape, jax.ShapeDtypeStruct((1, 2 * CLIPS * GROUPS), F32)),
        in_specs=[SMEM] + [VMEM] * 5,
        out_specs=[VMEM] * 2,
        input_output_aliases={5: 0},
        compiler_params=params(12),
        cost_estimate=cost(1 << 27, 1 << 20),
        name="columns",
    )(clips, weights, from_left, from_right, stats, conv)
    count = n_tm * n_row * n_col
    every = jnp.broadcast_to(stats[None], (count, *stats.shape))
    every = lax.all_to_all(every, ("tm", "row", "col"), 0, 0).reshape(count, -1)
    return pl.pallas_call(
        functools.partial(norm_kernel, H * n_row * W * n_col),
        out_shape=jax.ShapeDtypeStruct((F, H, W, COUT), BF),
        in_specs=[SMEM] + [VMEM] * 4,
        out_specs=HBM,
        scratch_shapes=[
            pltpu.VMEM((F, H, W, COUT), BF),
            pltpu.SemaphoreType.DMA((2 * F,)),
            pltpu.VMEM((F, 2, COUT), F32),
        ],
        compiler_params=params(12),
        cost_estimate=cost(1 << 24, 16 << 20),
        name="norm_silu",
    )(clips, every, norm_gain[None], norm_shift[None], conv)


def solution(mesh):
    return jax.shard_map(
        shards,
        mesh=mesh,
        in_specs=(P("tm", "row", "col", None), P(), P(), P(), P()),
        out_specs=P("tm", "row", "col", None),
        check_vma=False,
    )
```

```python
import functools

import jax
import jax.numpy as jnp
from jax import lax
from jax.experimental import pallas as pl
from jax.experimental.pallas import tpu as pltpu
from jax.sharding import PartitionSpec as P

COUT = 256
GROUPS = 32
CLIPS = 4
SHARE = COUT // GROUPS
F, H, W, C = 8, 8, 160, 128
C3 = 3 * C
BF, F32 = jnp.bfloat16, jnp.float32
VMEM = pl.BlockSpec(memory_space=pltpu.VMEM)
SMEM = pl.BlockSpec(memory_space=pltpu.SMEM)
HBM = pl.BlockSpec(memory_space=pltpu.HBM)


def clip_starts(frames_ref):
    starts = [0]
    for c in range(CLIPS - 1):
        starts.append(starts[-1] + frames_ref[c])
    return starts


def source(starts, first, f, k):
    g = first + f
    start = 0
    for s in starts[1:]:
        start = jnp.where(g >= s, s, start)
    return jnp.maximum(g - 2 + k, start) - first


def clip_index(starts, g):
    c = (g >= starts[1]).astype(jnp.int32)
    for s in starts[2:]:
        c = c + (g >= s).astype(jnp.int32)
    return c


def edges():
    row, col = lax.axis_index("row"), lax.axis_index("col")
    return row == 0, row == lax.axis_size("row") - 1, col == 0, col == lax.axis_size("col") - 1


def put_columns(xc, at, x, middle=True):
    _, _, left, right = edges()
    low = jnp.where(left, x[:, :1], jnp.zeros_like(x[:, :1]))
    high = jnp.where(right, x[:, -1:], jnp.zeros_like(x[:, -1:]))
    xc[(*at, slice(None), slice(None), slice(0, C))] = jnp.concatenate([low, x[:, :-1]], axis=1)
    if middle:
        xc[(*at, slice(None), slice(None), slice(C, 2 * C))] = x
    xc[(*at, slice(None), slice(None), slice(2 * C, 3 * C))] = jnp.concatenate([x[:, 1:], high], axis=1)


def time_weights(w_ref, taps):
    return w_ref[taps[0] * 3 * C3 : (taps[-1] + 1) * 3 * C3]


def inner_taps(frames, row, rows, w_ref, taps):
    parts = [
        frame[pl.ds(row - 1 + dy, rows)].reshape(rows * W, C3)
        for frame in frames
        for dy in range(3)
    ]
    lhs = jnp.concatenate(parts, axis=1)
    out = jnp.dot(lhs, time_weights(w_ref, taps), preferred_element_type=F32)
    return out.reshape(rows, W, COUT)


def times_zero_one(v, chosen):
    parts = []
    for _ in range(3):
        parts.append(v.astype(BF))
        v = v - parts[-1].astype(F32)
    out = jnp.dot(
        jnp.concatenate(parts, axis=0), chosen.astype(BF), preferred_element_type=F32
    ).reshape(3, v.shape[0], -1)
    return out[0] + (out[1] + out[2])


def cell_sum(v):
    sublane = lax.broadcasted_iota(jnp.int32, (1, 8, COUT), 1)
    v = jnp.concatenate(
        [
            jnp.where(sublane > 0, v[:, :8], 0.0),
            v[:, 8:-8],
            jnp.where(sublane < 7, v[:, -8:], 0.0),
        ],
        axis=1,
    )
    return jnp.sum(v.reshape(-1, COUT), axis=0, keepdims=True)


def add_stats(stats, f, v):
    off = v - stats[f, 0:1]
    stats[f, 1:2] += cell_sum(off)
    stats[f, 2:3] += cell_sum(off * off)


def start_stats(stats, f, v):
    stats[f] = jnp.zeros((8, COUT), F32)
    stats[f, 0:1] = cell_sum(v) * (1.0 / (v.shape[0] * (W - 2)))
    add_stats(stats, f, v)


def load_kernel(
    frames_hbm,
    x_hbm,
    w_hbm,
    tail,
    top_row,
    bottom_row,
    tail_top,
    tail_bottom,
    xc,
    w_ref,
    clips,
    x_sems,
    w_sem,
    c_sem,
):
    c_copy = pltpu.make_async_copy(frames_hbm, clips, c_sem)
    c_copy.start()

    own = xc.at[2:, :, :, C : 2 * C]

    def x_copy(f):
        return pltpu.make_async_copy(x_hbm.at[f], own.at[f], x_sems.at[f])

    for f in range(F):
        x_copy(f).start()
    w_copy = pltpu.make_async_copy(w_hbm, w_ref, w_sem)
    w_copy.start()

    def columns(f, carry):
        x_copy(f).wait()
        top_row[f] = own[f, 0]
        bottom_row[f] = own[f, H - 1]
        put_columns(xc, (f + 2,), own[f], middle=False)
        return carry

    lax.fori_loop(0, F, columns, 0)
    tail[...] = own[F - 2 :]
    tail_top[...] = own[F - 2 :, 0]
    tail_bottom[...] = own[F - 2 :, H - 1]
    w_copy.wait()
    c_copy.wait()


def inner_frame(f, first, starts, xc, w_ref, conv, stats):
    frames = [xc.at[source(starts, first, f, k) + 2] for k in range(2)] + [xc.at[f + 2]]
    for row in (1, 3, 5):
        out = inner_taps(frames, row, 2, w_ref, (0, 1, 2))
        conv[f, row : row + 2] = out
        (start_stats if row == 1 else add_stats)(stats, f, out)


def inner_kernel(frames, opening, frames_ref, xc, w_ref, *refs):
    conv, stats = refs[:2] if opening else refs[-3:-1]
    first = lax.axis_index("tm") * F
    starts = clip_starts(frames_ref)
    for f in frames:
        inner_frame(f, first, starts, xc, w_ref, conv, stats)
    if opening:
        for row in (1, 3, 5):
            conv[0, row : row + 2] = inner_taps([xc.at[2]], row, 2, w_ref, (2,))
            own = [xc.at[source(starts, first, 1, 1) + 2], xc.at[3]]
            conv[1, row : row + 2] = inner_taps(own, row, 2, w_ref, (1, 2))


def inner_part(frames, opening, clips, xc, weights, conv, stats, passed):
    out_shape = [pltpu.VMEM((F, H, W, COUT), F32), pltpu.VMEM((F, 8, COUT), F32)]
    held = [] if opening else [conv, stats, passed]
    if not opening:
        out_shape.append(pltpu.VMEM(passed.shape, passed.dtype))
    count = 3 * len(frames) + 3 * opening
    return pl.pallas_call(
        functools.partial(inner_kernel, frames, opening),
        out_shape=out_shape,
        in_specs=[SMEM] + [VMEM] * (2 + len(held)),
        out_specs=[VMEM] * len(out_shape),
        input_output_aliases={3 + i: i for i in range(len(held))},
        compiler_params=params(12),
        cost_estimate=cost(2 * count * 2 * W * 9 * C3 * COUT, 5 << 20),
        name="inner",
    )(clips, xc, weights, *held)


def strip_kernel(xc, before, above, below, above_before, below_before, low_out, high_out):
    top, bottom, _, _ = edges()
    for out, at, pick in ((low_out, 0, 0), (high_out, W - 16, 15)):

        def tile(ref, *where):
            return ref[(*where, slice(at, at + 16))].astype(F32)[pick : pick + 1]

        for f in range(F + 2):
            if f < 2:
                rows = [tile(before, f, r) for r in range(H)]
                over, under = tile(above_before, f), tile(below_before, f)
            else:
                g = f - 2
                rows = [
                    xc[f, r, at : at + 16, C : 2 * C].astype(F32)[pick : pick + 1]
                    for r in range(H)
                ]
                over, under = tile(above, g), tile(below, g)
            head = jnp.where(top, rows[0], over)
            tail = jnp.where(bottom, rows[-1], under)
            pad = jnp.zeros((16 - H - 2, C), F32)
            out[f] = jnp.concatenate([head, *rows, tail, pad], axis=0).astype(BF)


def outer_kernel(
    frames_ref,
    w_ref,
    before,
    above,
    below,
    above_before,
    below_before,
    arrived,
    xc_in,
    conv_in,
    stats_in,
    xc,
    conv,
    stats,
    rims,
):
    del arrived, xc_in, conv_in, stats_in
    first = lax.axis_index("tm") * F
    starts = clip_starts(frames_ref)
    top, bottom, _, _ = edges()

    def fill_rims(ref, at, own, over, under):
        rim = jnp.stack([jnp.where(top, own[0], over), jnp.where(bottom, own[H - 1], under)])
        put_columns(ref, (at,), rim)

    def outer_rows(f):
        parts = []
        for k in range(3):
            s = source(starts, first, f, k) + 2
            frame, rim = xc.at[s], rims.at[s]
            upper = [rim[0], frame[0], frame[1]]
            lower = [frame[H - 2], frame[H - 1], rim[1]]
            parts += [jnp.concatenate([u, v], axis=0) for u, v in zip(upper, lower)]
        lhs = jnp.concatenate(parts, axis=1)
        out = jnp.dot(lhs, w_ref[...], preferred_element_type=F32).reshape(2, W, COUT)
        conv[f, 0] = out[0]
        conv[f, H - 1] = out[1]
        return out

    for f in range(2):
        put_columns(xc, (f,), before[f])
        fill_rims(rims, f, before.at[f], above_before[f], below_before[f])
    for f in range(F):
        fill_rims(rims, f + 2, xc.at[f + 2, :, :, C : 2 * C], above[f], below[f])
    for f in range(2, F):
        add_stats(stats, f, outer_rows(f))
    for f in range(2):
        start_stats(stats, f, outer_rows(f))

    def first_frames(i, carry):
        row = 1 + 2 * i
        for f, taps in ((0, (0, 1)), (1, (0,))):
            frames = [xc.at[source(starts, first, f, k) + 2] for k in taps]
            out = conv[f, pl.ds(row, 2)] + inner_taps(frames, row, 2, w_ref, taps)
            conv[f, pl.ds(row, 2)] = out
            add_stats(stats, f, out)
        return carry

    lax.fori_loop(0, 3, first_frames, 0, unroll=3)


def column_kernel(frames_ref, w_ref, low_ref, high_ref, stats_ref, conv_in, conv, sums):
    del conv_in
    first = lax.axis_index("tm") * F
    starts = clip_starts(frames_ref)
    _, _, left, right = edges()
    total, square = [], []
    pivot = jnp.concatenate([stats_ref[f, 0:1] for f in range(F)], axis=0)
    total = jnp.concatenate([stats_ref[f, 1:2] for f in range(F)], axis=0)
    square = jnp.concatenate([stats_ref[f, 2:3] for f in range(F)], axis=0)
    for ref, edge, dx, at in ((low_ref, left, 0, 0), (high_ref, right, 2, W - 1)):
        lhs = []
        for f in range(F):
            parts = []
            for k in range(3):
                strip = ref[source(starts, first, f, k) + 2].astype(F32)
                strip = jnp.where(edge, 0.0, strip)
                parts += [strip[dy : dy + H] for dy in range(3)]
            lhs.append(jnp.concatenate(parts, axis=1))
        lhs = jnp.concatenate(lhs, axis=0).astype(BF)
        weights = jnp.concatenate(
            [w_ref[(t * 3 + dx) * C : (t * 3 + dx + 1) * C] for t in range(9)], axis=0
        )
        out = jnp.dot(lhs, weights, preferred_element_type=F32)
        added, added_square = [], []
        for f in range(F):
            column = jnp.concatenate([conv[f, r, at : at + 1] for r in range(H)], axis=0)
            column = column + out[f * H : (f + 1) * H]
            for r in range(H):
                conv[f, r, at : at + 1] = column[r : r + 1]
            off = column - pivot[f : f + 1]
            added.append(jnp.sum(off, axis=0, keepdims=True))
            added_square.append(jnp.sum(off * off, axis=0, keepdims=True))
        total = total + jnp.concatenate(added, axis=0)
        square = square + jnp.concatenate(added_square, axis=0)

    cells = float(H * W)
    mean = pivot + total * (1.0 / cells)
    square = square - total * total * (1.0 / cells)
    channel = lax.broadcasted_iota(jnp.int32, (COUT, COUT), 0) // SHARE
    same_group = channel == lax.broadcasted_iota(jnp.int32, (COUT, COUT), 1) // SHARE
    grouped = times_zero_one(mean, same_group)
    frame_row = lax.broadcasted_iota(jnp.int32, (F, COUT), 0)
    clip = clip_index(starts, first + frame_row)
    clip_sum = clip_count = jnp.zeros((F, COUT), F32)
    for f in range(F):
        same = clip == clip[f : f + 1]
        clip_sum = clip_sum + jnp.where(same, grouped[f : f + 1], 0.0)
        clip_count = clip_count + jnp.where(same, float(SHARE), 0.0)
    centre = clip_sum / clip_count
    off = mean - centre
    square = square + cells * (off * off)
    lane = lax.broadcasted_iota(jnp.int32, (COUT, CLIPS * GROUPS), 1)
    pick = lax.broadcasted_iota(jnp.int32, (COUT, CLIPS * GROUPS), 0) // SHARE == lane % GROUPS
    mine = lax.broadcasted_iota(jnp.int32, (F, CLIPS * GROUPS), 1) // GROUPS
    mine = mine == clip[:, : CLIPS * GROUPS]
    packed = times_zero_one(jnp.concatenate([mean * cells, square], axis=0), pick)
    for i in range(2):
        value = jnp.where(mine, packed[i * F : (i + 1) * F], 0.0)
        value = jnp.sum(value, axis=0, keepdims=True)
        sums[:, i * CLIPS * GROUPS : (i + 1) * CLIPS * GROUPS] = value


def norm_kernel(cells, frames_ref, all_ref, gain, shift, conv, out_ref, held, sems, per_frame):
    first = lax.axis_index("tm") * F
    starts = clip_starts(frames_ref)
    lanes = CLIPS * GROUPS
    count = all_ref.shape[0]
    value = all_ref[...]
    total, spread = value[:, :lanes], value[:, lanes:]
    which = lax.broadcasted_iota(jnp.int32, (count, lanes), 1) // GROUPS
    begin, length = jnp.zeros_like(which), jnp.zeros_like(which)
    for c in range(CLIPS):
        begin = jnp.where(which == c, starts[c], begin)
        length = jnp.where(which == c, frames_ref[c], length)
    slab = lax.broadcasted_iota(jnp.int32, (count, lanes), 0) // (count // lax.axis_size("tm")) * F
    part = jnp.minimum(slab + F, begin + length) - jnp.maximum(slab, begin)
    part = jnp.maximum(part, 0).astype(F32) * float(H * W * SHARE)
    whole = length[:1].astype(F32) * float(cells * SHARE)
    mean = jnp.sum(total, axis=0, keepdims=True) / whole
    off = total / jnp.maximum(part, 1.0) - mean
    var = jnp.sum(spread + part * (off * off), axis=0, keepdims=True) / whole
    var = var + 1e-06
    scale = lax.rsqrt(var)
    scale = scale * (1.5 - 0.5 * var * scale * scale)

    frame_row = lax.broadcasted_iota(jnp.int32, (F, lanes), 0)
    mine = clip_index(starts, first + frame_row)
    mine = mine == lax.broadcasted_iota(jnp.int32, (F, lanes), 1) // GROUPS
    lane = lax.broadcasted_iota(jnp.int32, (lanes, COUT), 0) % GROUPS
    chosen = lane == lax.broadcasted_iota(jnp.int32, (lanes, COUT), 1) // SHARE
    both = [jnp.where(mine, v, 0.0) for v in (mean, scale)]
    both = times_zero_one(jnp.concatenate(both, axis=0), chosen)
    mean, scale = both[:F], both[F:] * (0.5 * gain[...])
    offset = 0.5 * shift[...] - mean * scale

    def out_copy(f):
        f, h = f // 2, f % 2 * (H // 2)
        rows = (f, pl.ds(h, H // 2))
        return pltpu.make_async_copy(held.at[rows], out_ref.at[rows], sems.at[2 * f + h // (H // 2)])

    for f in range(F):
        per_frame[f] = jnp.concatenate([scale[f : f + 1], offset[f : f + 1]], axis=0)

    def half_frame(i, carry):
        f = i // 2
        for r in range(H // 2):
            h = i % 2 * (H // 2) + r
            u = conv[f, h] * per_frame[f, 0:1] + per_frame[f, 1:2]
            held[f, h] = (u + u * jnp.tanh(u)).astype(BF)
        out_copy(i).start()
        return carry

    lax.fori_loop(0, 2 * F, half_frame, 0)
    for i in range(2 * F):
        out_copy(i).wait()


def params(mib):
    return pltpu.CompilerParams(vmem_limit_bytes=mib << 20)


def cost(flops, moved):
    return pl.CostEstimate(flops=flops, bytes_accessed=moved, transcendentals=0)


def shards(frames_in, clip_frames, conv_weight, norm_gain, norm_shift):
    n_tm, n_row, n_col = (lax.axis_size(a) for a in ("tm", "row", "col"))
    weights = conv_weight.reshape(27 * C, COUT)
    tail, top_row, bottom_row, tail_top, tail_bottom, xc, weights, clips = pl.pallas_call(
        load_kernel,
        out_shape=[pltpu.VMEM((2, H, W, C), BF)]
        + [pltpu.VMEM((F, W, C), BF)] * 2
        + [pltpu.VMEM((2, W, C), BF)] * 2
        + [pltpu.VMEM((F + 2, H, W, C3), BF), pltpu.VMEM((27 * C, COUT), BF)]
        + [pltpu.SMEM((CLIPS,), jnp.int32)],
        in_specs=[HBM] * 3,
        out_specs=[VMEM] * 7 + [SMEM],
        scratch_shapes=[
            pltpu.SemaphoreType.DMA((F,)),
            pltpu.SemaphoreType.DMA,
            pltpu.SemaphoreType.DMA,
        ],
        compiler_params=params(50),
        name="load",
    )(clip_frames, frames_in, weights)
    down = [(i, (i + 1) % n_row) for i in range(n_row)]
    up = [(j, i) for i, j in down]
    later = [(t, (t + 1) % n_tm) for t in range(n_tm)]

    def diagonal(pairs):
        return [(t * n_row + i, u * n_row + j) for t, u in later for i, j in pairs]

    conv_shape = pltpu.VMEM((F, H, W, COUT), F32)
    xc_shape = pltpu.VMEM((F + 2, H, W, C3), BF)
    stats_shape = pltpu.VMEM((F, 8, COUT), F32)
    macs = W * 9 * C3 * COUT
    part = lambda *args: inner_part(args[0], args[1], clips, xc, weights, *args[2:])
    above = lax.ppermute(bottom_row, "row", down)
    below = lax.ppermute(top_row, "row", up)
    before = lax.ppermute(tail, "tm", later)
    above_before = lax.ppermute(tail_bottom, ("tm", "row"), diagonal(down))
    below_before = lax.ppermute(tail_top, ("tm", "row"), diagonal(up))
    conv, stats = part((2, 3, 4, 5, 6), True, None, None, None)
    low, high = pl.pallas_call(
        strip_kernel,
        out_shape=[pltpu.VMEM((F + 2, 16, C), BF)] * 2,
        in_specs=[VMEM] * 6,
        out_specs=[VMEM] * 2,
        compiler_params=params(8),
        cost_estimate=cost(1 << 20, 1 << 16),
        name="strips",
    )(xc, before, above, below, above_before, below_before)
    onward = [(i, (i + 1) % n_col) for i in range(n_col)]
    from_left = lax.ppermute(high, "col", onward)
    conv, stats, low = part((7,), False, conv, stats, low)
    from_right = lax.ppermute(low, "col", [(j, i) for i, j in onward])
    _, conv, stats = pl.pallas_call(
        outer_kernel,
        out_shape=(xc_shape, conv_shape, stats_shape),
        in_specs=[SMEM] + [VMEM] * 10,
        out_specs=[VMEM] * 3,
        input_output_aliases={8: 0, 9: 1, 10: 2},
        scratch_shapes=[pltpu.VMEM((F + 2, 2, W, C3), BF)],
        compiler_params=params(18),
        cost_estimate=cost(2 * 22 * macs, 5 << 20),
        name="outer",
    )(clips, weights, before, above, below, above_before, below_before, from_left, xc, conv, stats)
    conv, stats = pl.pallas_call(
        column_kernel,
        out_shape=(conv_shape, jax.ShapeDtypeStruct((1, 2 * CLIPS * GROUPS), F32)),
        in_specs=[SMEM] + [VMEM] * 5,
        out_specs=[VMEM] * 2,
        input_output_aliases={5: 0},
        compiler_params=params(12),
        cost_estimate=cost(1 << 27, 1 << 20),
        name="columns",
    )(clips, weights, from_left, from_right, stats, conv)
    count = n_tm * n_row * n_col
    every = jnp.broadcast_to(stats[None], (count, *stats.shape))
    every = lax.all_to_all(every, ("tm", "row", "col"), 0, 0).reshape(count, -1)
    return pl.pallas_call(
        functools.partial(norm_kernel, H * n_row * W * n_col),
        out_shape=jax.ShapeDtypeStruct((F, H, W, COUT), BF),
        in_specs=[SMEM] + [VMEM] * 4,
        out_specs=HBM,
        scratch_shapes=[
            pltpu.VMEM((F, H, W, COUT), BF),
            pltpu.SemaphoreType.DMA((2 * F,)),
            pltpu.VMEM((F, 2, COUT), F32),
        ],
        compiler_params=params(12),
        cost_estimate=cost(1 << 24, 16 << 20),
        name="norm_silu",
    )(clips, every, norm_gain[None], norm_shift[None], conv)


def solution(mesh):
    return jax.shard_map(
        shards,
        mesh=mesh,
        in_specs=(P("tm", "row", "col", None), P(), P(), P(), P()),
        out_specs=P("tm", "row", "col", None),
        check_vma=False,
    )
```
